512 devices in a mesh: group: 8 (over z_lo), member: 64 (over x, z_hi, y, core).
Axes of the slice: x: 4, y: 4, z: 16 (z_hi: 2, z_lo: 8; z = z_hi * 8 + z_lo), core: 2. Of those that a mesh axis runs over, the one named last changes fastest.
Arguments:
- replay_embed: bfloat16 [16384, 24, 1024], P(('group', 'member')), may hold values from -6 to 6
- replay_steps: bfloat16 [16384, 2, 24], P(('group', 'member')), as said below
- replay_actions: int32 [16384, 24], P(('group', 'member')), may hold values from 0 to 17
- replay_lengths: int32 [16384], P(('group', 'member')), may hold values from 1 to 24, as said below
- sample_owner: int32 [16384, 1], P(('group', 'member')), may hold values from 0 to 63; in each aligned block of 32 rows (0 to 31, 32 to 63, ...) no two rows name the same one
- sample_slot: int32 [16384], P(('group', 'member')), may hold values from 0 to 31
- sample_weight: float32 [16384], P(('group', 'member')), may hold values from 0.1 to 1
- norm_gain: float32 [1024], replicated
- w_query: bfloat16 [1024, 512], P('member')
- w_key: bfloat16 [1024, 512], P('member')
- w_value: bfloat16 [1024, 512], P('member'), may hold values from -0.1875 to 0.1875
- w_out: bfloat16 [512, 1024], P('member'), may hold values from -0.25 to 0.25
- q_head: bfloat16 [1024, 18], replicated, may hold values from -0.1875 to 0.1875
- policy_head: bfloat16 [1024, 18], replicated
Outputs:
- grad_value: float32 [1024, 512], P('member')
- grad_out: float32 [512, 1024], P('member')
The draws below stay inside these ranges and needn't reach their ends.
Inputs may be any that keep to these rules, and one draw needn't show every extreme that they name: `sample_owner`: the member of the row's own learner group that holds the sampled sequence; among the 32 rows of one device no member is named more than 1 times. `replay_lengths`: steps from a sequence's length on are padding. `replay_steps`: row 0 holds rewards, row 1 the behaviour policy's probability of the taken action, positive and at most 1.
All inputs are finite; a program needn't handle non-finite values.
Results may differ from the reference program's by a relative error of at most 0.0073.
Values may be sent and summed in bfloat16 or wider, within the bound.
No kernel may reach another device: no remote copies, remote signals or barrier semaphores. Data moves between devices by JAX's collectives and lax.ppermute only.
A program may use at most 64 MiB of HBM per device.

```python
import math
import jax
import jax.numpy as jnp
import numpy as np
from jax import lax

D = 1024
HEADS = 4
HEAD_DIM = 128
ACTIONS = 18
STEPS = 24
SEQ_DEV = 32
SLOTS = 32
ATT_WIDTH = 512
CAP = 1
ROWS = 16384
STORE = 16384
N_MEMBER = 64


def shared_base(key):
    return jax.random.normal(key, (D, HEADS * HEAD_DIM), jnp.float32)


def draw_replay_steps(key, part):
    key = jax.random.fold_in(key, 11)
    key_reward, key_level, key_jitter = jax.random.split(key, 3)
    level = jax.random.uniform(key_level, (STORE, 1, 1), jnp.float32, math.log(3e-05), 0.0)
    rewards = jax.random.normal(key_reward, (STORE, 1, STEPS), jnp.float32)
    jitter = jax.random.uniform(key_jitter, (STORE, 1, STEPS), jnp.float32, -0.5, 0.5)
    probs = jnp.minimum(1.0, jnp.exp(level + jitter))
    return jnp.concatenate([rewards, probs], axis=1).astype(jnp.bfloat16)


def draw_replay_lengths(key, part):
    key = jax.random.fold_in(key, 12)
    drawn = jax.random.randint(key, (STORE,), 1, STEPS + 1)
    position = jnp.arange(STORE)
    return jnp.where(position % 3 == 0, STEPS, drawn).astype(jnp.int32)


def draw_norm_gain(key, part):
    key = jax.random.fold_in(key, 13)
    ramp = 0.5 + jnp.arange(D, dtype=jnp.float32) / D
    factor = jax.random.uniform(key, (D,), jnp.float32, 0.8, 1.2)
    return ramp * factor


def draw_w_key(key, part):
    base = shared_base(key)
    return (base / math.sqrt(D)).astype(jnp.bfloat16)


def draw_w_query(key, part):
    key = jax.random.fold_in(key, 22)
    key_fresh = jax.random.fold_in(key, 0)
    fresh = jax.random.normal(key_fresh, (D, HEADS * HEAD_DIM), jnp.float32)
    return (fresh / math.sqrt(D)).astype(jnp.bfloat16)


def draw_policy_head(key, part):
    key = jax.random.fold_in(key, 31)
    key_entries = jax.random.fold_in(key, 0)
    entries = jax.random.normal(key_entries, (D, ACTIONS), jnp.float32)
    return (entries * 2.0 / math.sqrt(D)).astype(jnp.bfloat16)


def with_ends(values, key, low, high):
    dims = values.shape
    index_at = [jax.random.randint(jax.random.fold_in(key, axis), (), 0, dims[axis]) for axis in range(len(dims))]
    values = values.at[tuple(index_at)].set(low)
    longest = dims.index(max(dims))
    index_at[longest] = (index_at[longest] + 1) % dims[longest]
    return values.at[tuple(index_at)].set(high)


def block_scale(own_key, shape, pieces, smallest, high):
    loudness = 1.0
    for axis_at, blocks in pieces:
        steps = jax.random.uniform(jax.random.fold_in(jax.random.fold_in(own_key, 6), axis_at), (blocks,), jnp.float32, smallest / len(pieces), high / len(pieces))
        loudness = loudness * jnp.repeat(jnp.exp(steps), shape[axis_at] // blocks).reshape((-1,) + (1,) * (len(shape) - 1 - axis_at))
    return loudness


def assign_block(own_key, own, number, rows, amount, top, bound, slope):
    order = jax.random.permutation(own_key, amount)
    heavy_load, usual = portions_of(amount, rows * top, bound, slope, True), portions_of(amount, rows * top, bound, slope, False)
    places = jnp.arange(amount)

    def named(sizes, offset_by):
        used = int((sizes > 0).sum())
        fixed = max(1, used // 4)
        shifted = fixed + (places - fixed + offset_by * (used - fixed)) % max(1, amount - fixed)
        return jnp.zeros((amount,), jnp.int32).at[order[jnp.where(places < fixed, places, shifted)]].set(jnp.asarray(sizes, jnp.int32))

    sizes = jnp.where(number % 4 == 0, named(heavy_load, number // 4), named(usual, number - number // 4 - 1))
    mixed = jax.random.permutation(jax.random.fold_in(own, 3), amount)
    source_of, sink = mixed[0:amount // 2 * 2:2], mixed[1:amount // 2 * 2:2]
    room = jnp.minimum(sizes[source_of] - 1, bound - sizes[sink]) // 2
    room = jnp.where((source_of == order[0]) | (sink == order[0]) | (sizes[sink] == 0), 0, jnp.maximum(room, 0))
    shifted = jax.random.randint(jax.random.fold_in(own, 4), (amount // 2,), 0, 1 << 20) % (room + 1)
    sizes = sizes.at[source_of].add(-shifted).at[sink].add(shifted)
    items = jnp.searchsorted(jnp.cumsum(sizes), jnp.arange(rows * top), side="right").astype(jnp.int32)
    listing = items.reshape(top, rows).T
    listing = listing[jax.random.permutation(jax.random.fold_in(own, 1), rows)]
    offset_by = jax.random.randint(jax.random.fold_in(own, 2), (rows, 1), 0, top)
    return jnp.take_along_axis(listing, (jnp.arange(top)[None, :] + offset_by) % top, axis=1)


def portions_of(amount, total, bound, lean, full):
    portions = [(1 << 20) // math.isqrt(grade ** lean) + 1 for grade in range(1, amount + 1)]
    largest = bound if full else min(bound, max(-(-total // amount), total * portions[0] // sum(portions)))
    least = 1 if total - largest >= amount - 1 else 0
    holding, rest = [largest] + [least] * (amount - 1), total - largest - least * (amount - 1)
    while rest > 0:
        free = [i for i in range(1, amount) if holding[i] < largest] or [i for i in range(1, amount) if holding[i] < bound]
        whole, left = sum([portions[i] for i in free]), rest
        for i in free:
            more = min(bound - holding[i], max(1, left * portions[i] // whole), rest)
            holding[i] = holding[i] + more
            rest = rest - more
    return np.array(holding)


def gaussian(stream_key, extent, scale, bound, pieces=(), kind=jnp.bfloat16):
    level = block_scale(stream_key, extent, pieces, -0.22, 0.18) if pieces else 1.0
    values = jax.random.normal(stream_key, extent, jnp.float32) * scale * level
    return jnp.minimum(jnp.maximum(values, -bound), bound).astype(kind)


def setup_inputs(seed: int = 0) -> dict:
    key_list = jax.random.split(jax.random.key(seed), 15)
    replay_embed = gaussian(key_list[0], (STORE, STEPS, D), 1.0, 6.0, ((0, 512),))
    replay_steps = draw_replay_steps(jax.random.fold_in(key_list[14], 71), 0)
    replay_actions = with_ends(jax.random.randint(key_list[2], (STORE, STEPS), 0, ACTIONS), jax.random.fold_in(key_list[2], 1), 0, ACTIONS - 1).astype(jnp.int32)
    replay_lengths = draw_replay_lengths(jax.random.fold_in(key_list[14], 71), 0)
    sample_owner_keys = jax.random.split(jax.random.fold_in(key_list[4], 1), ROWS // SEQ_DEV)
    sample_owner_turns = jax.random.permutation(jax.random.fold_in(key_list[4], 3), ROWS // SEQ_DEV)
    sample_owner = jax.vmap(lambda own, number: assign_block(jax.random.fold_in(key_list[4], 2), own, number, SEQ_DEV, N_MEMBER, 1, CAP, 2))(sample_owner_keys, sample_owner_turns).reshape((ROWS, 1))
    sample_slot = with_ends(jax.random.randint(key_list[5], (ROWS,), 0, SLOTS), jax.random.fold_in(key_list[5], 1), 0, SLOTS - 1).astype(jnp.int32)
    sample_weight = jnp.clip(jnp.exp(math.log(1.0) - 2.3025851 * jax.random.uniform(key_list[6], (ROWS,), jnp.float32) ** block_scale(key_list[6], (ROWS,), ((0, 512),), -0.2, 0.2)), 0.1, 1.0)
    norm_gain = draw_norm_gain(jax.random.fold_in(key_list[14], 71), 0)
    w_query = draw_w_query(jax.random.fold_in(key_list[14], 71), 0)
    w_key = draw_w_key(jax.random.fold_in(key_list[14], 71), 0)
    w_value = gaussian(key_list[10], (D, ATT_WIDTH), D ** -0.5, 0.1875, ((0, 64),))
    w_out = gaussian(key_list[11], (ATT_WIDTH, D), ATT_WIDTH ** -0.5, 0.25, ((0, 64),))
    q_head = gaussian(key_list[12], (D, ACTIONS), D ** -0.5, 0.1875)
    policy_head = draw_policy_head(jax.random.fold_in(key_list[14], 71), 0)
    return {"replay_embed": replay_embed, "replay_steps": replay_steps, "replay_actions": replay_actions, "replay_lengths": replay_lengths, "sample_owner": sample_owner, "sample_slot": sample_slot, "sample_weight": sample_weight, "norm_gain": norm_gain, "w_query": w_query, "w_key": w_key, "w_value": w_value, "w_out": w_out, "q_head": q_head, "policy_head": policy_head}


trace_lambda = 0.95
discount = 0.997
clip_norm = 1024.0

def normalize_rows(embeds, gain_row):
    values = embeds.astype(jnp.float32)
    meansq = lax.optimization_barrier(jnp.mean(values * values, axis=-1, keepdims=True))
    return (values * lax.rsqrt(meansq + 1e-06) * gain_row).astype(jnp.bfloat16)

def retrace_grad(q_values, policy, actions, step_data, lengths, weights):
    num_seq, seq_len, action_count = q_values.shape
    picker = (actions[..., None] == jnp.arange(action_count)[None, None, :]).astype(jnp.float32)
    rewards = step_data[:, 0, :].astype(jnp.float32)
    behaviour = step_data[:, 1, :].astype(jnp.float32)
    values = lax.optimization_barrier(jnp.sum(policy * q_values, axis=-1))
    taken_q = lax.optimization_barrier(jnp.sum(picker * q_values, axis=-1))
    traces = trace_lambda * jnp.minimum(1.0, lax.optimization_barrier(jnp.sum(picker * policy, axis=-1)) / behaviour)
    positions = jnp.arange(seq_len)
    live_mask = (positions[None, :] < lengths[:, None]).astype(jnp.float32)
    onward = (positions[None, :] + 1 < lengths[:, None]).astype(jnp.float32)
    padding = jnp.zeros((num_seq, 1), jnp.float32)
    next_values = jnp.concatenate([values[:, 1:], padding], axis=1)
    next_traces = jnp.concatenate([traces[:, 1:], padding], axis=1)
    next_taken = jnp.concatenate([taken_q[:, 1:], padding], axis=1)

    def stepper(later_target, inputs):
        reward_now, continues, value_next, trace_next, taken_next = inputs
        target_now = reward_now + discount * continues * (value_next + trace_next * (later_target - taken_next))
        return (target_now, target_now)
    last_target, targets = lax.scan(stepper, jnp.zeros((num_seq,), jnp.float32), (rewards.T, onward.T, next_values.T, next_traces.T, next_taken.T), reverse=True)
    errors = weights[:, None] * live_mask * (taken_q - targets.T)
    return errors[..., None] * picker

def sequence_grads(embeds, step_data, actions, lengths, weights, gain_row, w_query, w_key, w_value, w_out, q_head, policy_head):
    num_seq, seq_len, features = embeds.shape
    normed = normalize_rows(embeds, gain_row).reshape(num_seq * seq_len, features)

    def project(matrix):
        return jnp.dot(normed, matrix, preferred_element_type=jnp.float32).astype(jnp.bfloat16).reshape(num_seq, seq_len, -1, HEAD_DIM)
    queries = project(w_query)
    keys_all = project(w_key)
    values_all = project(w_value)
    scores = jnp.einsum('bqhe,bkhe->bhqk', queries.astype(jnp.float32), keys_all.astype(jnp.float32)) * HEAD_DIM ** (-0.5)
    positions = jnp.arange(seq_len)
    causal = positions[None, :] <= positions[:, None]
    allowed = causal[None, None, :, :] & (positions[None, None, None, :] < lengths[:, None, None, None])
    scores = jnp.where(allowed, scores, -1e+30)
    row_peak = lax.optimization_barrier(jnp.max(scores, axis=-1, keepdims=True))
    weights_exp = jnp.where(allowed, jnp.exp(scores - row_peak), 0.0)
    attn_probs = (weights_exp / lax.optimization_barrier(jnp.sum(weights_exp, axis=-1, keepdims=True))).astype(jnp.bfloat16)
    mixed_heads = jnp.einsum('bhqk,bkhe->bqhe', attn_probs.astype(jnp.float32), values_all.astype(jnp.float32))
    mixed_heads = mixed_heads.astype(jnp.bfloat16).reshape(num_seq * seq_len, -1)
    hidden = embeds.reshape(num_seq * seq_len, features).astype(jnp.float32) + jnp.dot(mixed_heads, w_out, preferred_element_type=jnp.float32)
    hidden = hidden.astype(jnp.bfloat16)
    q_values = jnp.dot(hidden, q_head, preferred_element_type=jnp.float32)
    policy = jax.nn.softmax(jnp.dot(hidden, policy_head, preferred_element_type=jnp.float32), axis=-1)
    d_qvalues = retrace_grad(q_values.reshape(num_seq, seq_len, -1), policy.reshape(num_seq, seq_len, -1), actions, step_data, lengths, weights).reshape(num_seq * seq_len, -1)
    d_hidden = jnp.dot(d_qvalues, q_head.astype(jnp.float32).T, precision=lax.Precision.HIGHEST).astype(jnp.bfloat16)
    grad_out = lax.dot_general(mixed_heads, d_hidden, (((0,), (0,)), ((), ())), preferred_element_type=jnp.float32)
    d_mixed = lax.dot_general(d_hidden, w_out, (((1,), (1,)), ((), ())), preferred_element_type=jnp.float32)
    d_mixed = d_mixed.astype(jnp.bfloat16).reshape(num_seq, seq_len, -1, HEAD_DIM)
    d_value = jnp.einsum('bhqk,bqhe->bkhe', attn_probs.astype(jnp.float32), d_mixed.astype(jnp.float32))
    d_value = d_value.astype(jnp.bfloat16).reshape(num_seq * seq_len, -1)
    grad_value = lax.dot_general(normed, d_value, (((0,), (0,)), ((), ())), preferred_element_type=jnp.float32)
    return (grad_value, grad_out)

def reference(replay_embed, replay_steps, replay_actions, replay_lengths, sample_owner, sample_slot, sample_weight, norm_gain, w_query, w_key, w_value, w_out, q_head, policy_head):
    row_index = jnp.arange(ROWS, dtype=jnp.int32)
    group_of = row_index // (N_MEMBER * SEQ_DEV)
    source = ((group_of * N_MEMBER + sample_owner[:, 0]) * SLOTS + sample_slot).astype(jnp.int32)
    blocks = ROWS // SEQ_DEV

    def accumulate(totals, inputs):
        picked, weights = inputs
        partial_sums = sequence_grads(jnp.take(replay_embed, picked, axis=0), jnp.take(replay_steps, picked, axis=0), jnp.take(replay_actions, picked, axis=0), jnp.take(replay_lengths, picked, axis=0), weights, norm_gain, w_query, w_key, w_value, w_out, q_head, policy_head)
        return ((totals[0] + partial_sums[0], totals[1] + partial_sums[1]), None)
    starting = (jnp.zeros((D, ATT_WIDTH), jnp.float32), jnp.zeros((ATT_WIDTH, D), jnp.float32))
    sums, unused = lax.scan(accumulate, starting, (source.reshape(blocks, SEQ_DEV), sample_weight.reshape(blocks, SEQ_DEV)))
    squares = jnp.sum(sums[0] * sums[0]) + jnp.sum(sums[1] * sums[1])
    clip_scale = jnp.minimum(1.0, clip_norm / jnp.sqrt(squares))
    return (sums[0] * clip_scale, sums[1] * clip_scale)
```

```python
import jax
import jax.numpy as jnp
from jax import lax
from jax.experimental import pallas as pl
from jax.experimental.pallas import tpu as pltpu
from jax.sharding import Mesh
from jax.sharding import PartitionSpec as P

AXES = ("g", "x", "zh", "y", "c")
SHAPE = (8, 4, 2, 4, 2)
SWAP = [(0, 1), (1, 0)]
FOUR_AWAY = [(g * 2 + zh, (g + 4) % 8 * 2 + 1 - zh) for g in range(8) for zh in range(2)]

HEADS = 4
HEAD_DIM = 128
ACTIONS = 18
STEPS = 24
BLOCKS = 8
BLOCK = 96
PAD = 24
TILES = 13

trace_lambda = 0.95
discount = 0.997
clip_norm = 1024.0

F32 = jnp.float32
BF16 = jnp.bfloat16
HIGHEST = lax.Precision.HIGHEST
VMEM = pl.BlockSpec(memory_space=pltpu.VMEM)
SMEM = pl.BlockSpec(memory_space=pltpu.SMEM)


def call(kernel, out_shape, in_specs, scratch=(), flops=0, moved=0, limit=32):
    return pl.pallas_call(
        kernel,
        out_shape=out_shape,
        in_specs=in_specs,
        out_specs=jax.tree.map(lambda s: VMEM, out_shape),
        scratch_shapes=list(scratch),
        compiler_params=pltpu.CompilerParams(vmem_limit_bytes=limit * 1024 * 1024),
        cost_estimate=pl.CostEstimate(flops=flops, bytes_accessed=moved, transcendentals=0),
    )


def shape(dims, dtype=F32):
    return jax.ShapeDtypeStruct(dims, dtype)


def iota(dims, axis):
    return lax.broadcasted_iota(jnp.int32, dims, axis)


def dot_nt(a, b):
    return lax.dot_general(a, b, (((1,), (1,)), ((), ())), preferred_element_type=F32)


def split(values):
    high = values.astype(BF16).astype(F32)
    return high, values - high


def step_of(lanes):
    out = lanes
    for edge in (24, 48, 72, 96, 120):
        out = out - jnp.where(lanes >= edge, 24, 0)
    return out


def payload_kernel(w_query, w_key, w_value, w_out, heads, out):
    for mat, ref in enumerate((w_query, w_key, w_value)):
        for tile in range(4):
            out[mat * 4 + tile] = ref[:, tile * 128 : (tile + 1) * 128]
    high, low = split(jnp.dot(w_out[...], heads[...], preferred_element_type=F32))
    both = high + pltpu.roll(low, 48, 1)
    out[12] = jnp.concatenate([both, jnp.zeros((8, 128), F32)], axis=0).astype(BF16)


def norm_kernel(embeds, gain, heads, normed, base, q_rows):
    turned = heads[...].astype(F32).T
    row = iota((128, 1024), 0)
    q_rows[...] = jnp.where(row >= 96, pltpu.roll(jnp.where(row < PAD, turned, 0.0), 96, 0), 0.0)
    both = turned[:48].astype(BF16)
    base[...] = jnp.zeros_like(base)
    for b in range(BLOCKS):
        rows = embeds[b * BLOCK : (b + 1) * BLOCK, :]
        values = rows.astype(F32)
        meansq = jnp.mean(values * values, axis=-1, keepdims=True)
        normed[b * BLOCK : (b + 1) * BLOCK, :] = (
            values * lax.rsqrt(meansq + 1e-06) * gain[...]
        ).astype(BF16)
        base[b, :, :BLOCK] = dot_nt(both, rows)


def pack_kernel(zh_ref, own, other, keep, recv, out):
    zh = zh_ref[0]
    high, low = split(keep[...] + recv[...])
    zeros = jnp.zeros((8, 128), F32)
    first = jnp.where(zh == 0, own[12].astype(F32), other[12].astype(F32))
    second = jnp.where(zh == 0, other[12], own[12])
    for d in range(16):
        for k in range(12):
            out[d, zh * TILES + k] = own[k]
            out[d, (1 - zh) * TILES + k] = other[k]
        at = 2 * d
        rows = [high[at : at + 1], low[at : at + 1], high[at + 1 : at + 2], low[at + 1 : at + 2]]
        table = jnp.concatenate([zeros] + rows + [zeros[:4]], axis=0)
        out[d, 12] = (first + table).astype(BF16)
        out[d, TILES + 12] = second


def main_kernel(
    c_ref, normed, base, mine, theirs, aux, out, value_rows,
    wall, wo, qkv, probs, mixed, logits, dq, grad_n, grad_g,
):
    c = c_ref[0]

    def unpack(s, total):
        x, y = s >> 2, s & 3
        for zh in range(2):
            for ref, core in ((mine, c), (theirs, 1 - c)):
                m = ((x * 2 + zh) * 4 + y) * 2 + core
                rows = pl.ds(pl.multiple_of(m * 16, 16), 16)
                for tile in range(12):
                    wall[rows, tile * 128 : (tile + 1) * 128] = ref[s, zh * TILES + tile]
                last = ref[s, zh * TILES + 12].astype(F32)
                wo[pl.ds(pl.multiple_of(m * 8, 8), 8), :] = last[:8]
                if zh == 0:
                    total = total + last
        return total

    total = lax.fori_loop(0, 16, unpack, jnp.zeros((16, 128), F32))
    weights = jnp.where(c == 0, total[8:9] + total[9:10], total[10:11] + total[11:12])

    turned = wo[...].T
    both = turned[:96].astype(BF16)
    own_value = turned[:PAD] + turned[48 : 48 + PAD]
    head_of = iota((PAD, 512), 1) >> 7
    for h in range(HEADS):
        value_rows[h * PAD : (h + 1) * PAD, :] = jnp.where(head_of == h, own_value, 0.0)
    value_rows[HEADS * PAD :, :] = jnp.zeros((128 - HEADS * PAD, 512), F32)

    def project(n, carry):
        cols = pl.ds(pl.multiple_of(n * 256, 256), 256)
        qkv[:, cols] = jnp.dot(
            normed[...], wall[:, cols], preferred_element_type=F32
        ).astype(BF16)
        return carry

    lax.fori_loop(0, 6, project, 0)

    row, col = iota((BLOCK, BLOCK), 0), iota((BLOCK, BLOCK), 1)
    row_step, col_step = step_of(row), step_of(col)
    causal = (row - row_step == col - col_step) & (col_step <= row_step)
    logits[...] = base[...]

    def attend(b, carry):
        rows = pl.ds(pl.multiple_of(b * BLOCK, 32), BLOCK)
        lengths = aux[3, pl.ds(b, 1), :][:, :BLOCK].astype(jnp.int32)
        allowed = causal & (col_step < lengths)
        for h in range(HEADS):
            at = h * HEAD_DIM
            scores = dot_nt(qkv[rows, at : at + 128], qkv[rows, 512 + at : 640 + at])
            scores = jnp.where(allowed, scores * HEAD_DIM ** (-0.5), -1e30)
            peak = jnp.max(scores, axis=-1, keepdims=True)
            grown = jnp.where(allowed, jnp.exp(scores - peak), 0.0)
            weighed = (grown / jnp.sum(grown, axis=-1, keepdims=True)).astype(BF16)
            probs[b * HEADS + h] = weighed
            mixed[rows, at : at + 128] = jnp.dot(
                weighed, qkv[rows, 1024 + at : 1152 + at], preferred_element_type=F32
            ).astype(BF16)
        lifted = dot_nt(both, mixed[rows, :])
        logits[b, :, :BLOCK] = logits[b, :, :BLOCK] + lifted[:48] + lifted[48:]
        return carry

    lax.fori_loop(0, BLOCKS, attend, 0)

    action_row = iota((BLOCKS, PAD, 128), 1)
    real = action_row < ACTIONS
    qvals = logits[:, :PAD, :]
    raised = jnp.where(real, logits[:, PAD:, :], -1e30)
    raised = jnp.where(real, jnp.exp(raised - jnp.max(raised, axis=1, keepdims=True)), 0.0)
    policy = raised / jnp.sum(raised, axis=1, keepdims=True)
    picked = action_row == aux[2].astype(jnp.int32)[:, None, :]
    values = jnp.sum(policy * qvals, axis=1)
    taken = jnp.sum(jnp.where(picked, qvals, 0.0), axis=1)
    chosen = jnp.sum(jnp.where(picked, policy, 0.0), axis=1)
    behaviour = aux[1]
    traces = trace_lambda * jnp.where(chosen >= behaviour, 1.0, chosen / behaviour)
    lengths = aux[3].astype(jnp.int32)
    lane, block = iota((BLOCKS, 128), 1), iota((BLOCKS, 128), 0)
    step = step_of(lane)
    onward = step + 1 < lengths

    def later(array, count):
        return pltpu.roll(array, 128 - count, 1)

    next_traces = later(traces, 1)
    targets = aux[0] + jnp.where(
        onward, discount * (later(values, 1) - next_traces * later(taken, 1)), 0.0
    )
    factor = jnp.where(onward, discount * next_traces, 0.0)
    for count in (1, 2, 4, 8, 16):
        targets = targets + factor * later(targets, count)
        factor = factor * later(factor, count)

    by_block = jnp.where(lane >> 2 == block, weights, 0.0)
    slot, place = iota((128, 128), 0), iota((128, 128), 1)
    spread = jnp.where((slot & 3) * STEPS == place - step_of(place), 1.0, 0.0)
    row_weight = jnp.dot(by_block, spread, preferred_element_type=F32, precision=HIGHEST)
    live = (step < lengths) & (row_weight != 0.0)
    errors = jnp.where(live, row_weight * (taken - targets), 0.0)
    high, low = split(errors)
    dq[:, :PAD, :] = jnp.where(picked, high[:, None, :], 0.0).astype(BF16)
    dq[:, PAD:, :] = jnp.where(picked, low[:, None, :], 0.0).astype(BF16)

    grad_n[...] = jnp.zeros_like(grad_n)
    grad_g[...] = jnp.zeros_like(grad_g)

    def backward(b, carry):
        rows = pl.ds(pl.multiple_of(b * BLOCK, 32), BLOCK)
        given = dq[b][:, :BLOCK]
        parts = []
        for h in range(HEADS):
            both_parts = jnp.dot(given, probs[b * HEADS + h], preferred_element_type=F32)
            parts.append(both_parts[:PAD] + both_parts[PAD:])
        high, low = split(jnp.concatenate(parts, axis=0))
        stacked = jnp.concatenate([high, low], axis=0).astype(BF16)
        update = jnp.dot(stacked, normed[rows, :], preferred_element_type=F32)
        grad_n[:96, :] += update[:96] + update[96:]
        update = jnp.dot(given, mixed[rows, :], preferred_element_type=F32)
        grad_g[96 : 96 + PAD, :] += update[:PAD] + update[PAD:]
        return carry

    lax.fori_loop(0, BLOCKS, backward, 0)

    by_row, by_feature = grad_n[...].T, grad_g[...].T
    for p in range(32):
        x, y, core = p >> 3, (p >> 1) & 3, p & 1
        m0 = (x * 8 + y) * 2 + core
        m1 = m0 + 8
        upper = by_row[m0 * 16 : m0 * 16 + 16] + jnp.concatenate(
            [by_feature[m0 * 8 : m0 * 8 + 8], by_feature[m1 * 8 : m1 * 8 + 8]], axis=0
        )
        out[p] = jnp.concatenate([upper, by_row[m1 * 16 : m1 * 16 + 16]], axis=0).astype(out.dtype)


def grads_kernel(parts, value_rows, q_rows, grad_value, grad_out, squares):
    total = parts[0].astype(F32)
    for z in range(1, 16):
        total = total + parts[z].astype(F32)
    by_value = jnp.dot(total, value_rows[...], preferred_element_type=F32, precision=HIGHEST)
    by_out = jnp.dot(total[:16], q_rows[...], preferred_element_type=F32, precision=HIGHEST)
    grad_value[...] = by_value
    grad_out[...] = by_out
    sums = jnp.zeros((8, 128), F32)
    for array in (by_value * by_value, by_out * by_out):
        for r in range(0, array.shape[0], 8):
            for k in range(0, array.shape[1], 128):
                sums = sums + array[r : r + 8, k : k + 128]
    squares[...] = sums


def clip_kernel(zh_ref, squares, by_value, by_out, grad_value, grad_out):
    zh = zh_ref[0]
    total = jnp.sum(jnp.sum(squares[...], axis=0), keepdims=True)
    scale = jnp.minimum(1.0, clip_norm / jnp.sqrt(total))
    grad_value[...] = by_value[pl.ds(pl.multiple_of(zh * 16, 16), 16), :] * scale
    grad_out[...] = by_out[pl.ds(pl.multiple_of(zh * 8, 8), 8), :] * scale


def make_payload(w_query, w_key, w_value, w_out, heads):
    return call(payload_kernel, shape((TILES, 16, 128), BF16), [VMEM] * 5, flops=2 * 10**6, moved=10**5)(
        w_query, w_key, w_value, w_out, heads
    )


def make_normed(embeds, gain, heads):
    return call(
        norm_kernel,
        (shape((768, 1024), BF16), shape((BLOCKS, 48, 128)), shape((128, 1024))),
        [VMEM] * 3,
        flops=10**8,
        moved=4 * 10**6,
    )(embeds, gain, heads)


def make_message(zh, own, other, keep, recv):
    return call(
        pack_kernel, shape((16, 2 * TILES, 16, 128), BF16), [SMEM] + [VMEM] * 4, moved=2 * 10**6
    )(zh, own, other, keep, recv)


def make_sums(core, normed, base, mine, theirs, aux, dtype):
    return call(
        main_kernel,
        (shape((32, 32, 128), dtype), shape((128, 512))),
        [SMEM] + [VMEM] * 5,
        [
            pltpu.VMEM((1024, 1536), BF16),
            pltpu.VMEM((512, 128), F32),
            pltpu.VMEM((768, 1536), BF16),
            pltpu.VMEM((BLOCKS * HEADS, BLOCK, BLOCK), BF16),
            pltpu.VMEM((768, 512), BF16),
            pltpu.VMEM((BLOCKS, 48, 128), F32),
            pltpu.VMEM((BLOCKS, 48, 128), BF16),
            pltpu.VMEM((128, 1024), F32),
            pltpu.VMEM((128, 512), F32),
        ],
        flops=4 * 10**9,
        moved=10**7,
        limit=48,
    )(core, normed, base, mine, theirs, aux)


def make_grads(parts, value_rows, q_rows):
    return call(
        grads_kernel,
        (shape((32, 512)), shape((16, 1024)), shape((8, 128))),
        [VMEM] * 3,
        flops=10**7,
        moved=10**6,
    )(parts, value_rows, q_rows)


def make_clipped(zh, squares, by_value, by_out):
    return call(
        clip_kernel, (shape((16, 512)), shape((8, 1024))), [SMEM] + [VMEM] * 3, moved=2 * 10**5
    )(zh, squares, by_value, by_out)


def padded_heads(q_head, policy_head):
    width = ((0, 0), (0, PAD - ACTIONS))
    return jnp.concatenate(
        [jnp.pad(q_head, width), jnp.pad(policy_head, width), jnp.zeros((1024, 80), BF16)], axis=1
    )


def row_facts(replay_steps, replay_actions, replay_lengths):
    def lanes(array, fill):
        flat = array.astype(F32).reshape(BLOCKS, BLOCK)
        return jnp.pad(flat, ((0, 0), (0, 128 - BLOCK)), constant_values=fill)

    lengths = jnp.broadcast_to(replay_lengths[:, None], (32, STEPS))
    return jnp.stack([
        lanes(replay_steps[:, 0, :], 0.0),
        lanes(replay_steps[:, 1, :], 1.0),
        lanes(replay_actions, 0.0),
        lanes(lengths, 0.0),
    ])


def slot_weights(sample_owner, sample_slot, sample_weight, zh):
    owner = sample_owner[:, 0]
    place = (owner >> 4) * 8 + (owner & 7)
    half = (owner >> 3) & 1
    hit = (place[:, None, None] == jnp.arange(32)[None, :, None]) & (
        sample_slot[:, None, None] == jnp.arange(128)[None, None, :]
    )
    weights = jnp.where(hit, sample_weight[:, None, None], 0.0)
    stays = (half == zh)[:, None, None]
    return jnp.sum(jnp.where(stays, weights, 0.0), axis=0), jnp.sum(jnp.where(stays, 0.0, weights), axis=0)


def per_device(
    replay_embed,
    replay_steps,
    replay_actions,
    replay_lengths,
    sample_owner,
    sample_slot,
    sample_weight,
    norm_gain,
    w_query,
    w_key,
    w_value,
    w_out,
    q_head,
    policy_head,
):
    zh = lax.axis_index("zh").astype(jnp.int32)
    core = lax.axis_index("c").astype(jnp.int32)
    heads = padded_heads(q_head, policy_head)
    own = make_payload(w_query, w_key, w_value, w_out, heads)
    other = lax.ppermute(own, ("g", "zh"), FOUR_AWAY)
    keep, send = slot_weights(sample_owner, sample_slot, sample_weight, zh)
    recv = lax.ppermute(send, "zh", SWAP)
    normed, base, q_rows = make_normed(
        replay_embed.reshape(768, 1024), norm_gain.reshape(1, 1024), heads
    )
    aux = row_facts(replay_steps, replay_actions, replay_lengths)
    message = make_message(zh.reshape(1), own, other, keep, recv)
    mine = lax.all_to_all(message, ("x", "y"), split_axis=0, concat_axis=0, tiled=True)
    theirs = lax.ppermute(mine, "c", SWAP)
    sums, value_rows = make_sums(core.reshape(1), normed, base, mine, theirs, aux, F32)
    parts = lax.all_to_all(sums, ("x", "y", "c"), split_axis=0, concat_axis=0, tiled=True)
    plane = jnp.sum(parts.astype(F32), axis=0)
    copies = jnp.broadcast_to(plane[None], (16, 32, 128))
    planes = lax.all_to_all(copies, ("zh", "g"), split_axis=0, concat_axis=0, tiled=True)
    by_value, by_out, squares = make_grads(planes, value_rows, q_rows)
    squares = lax.all_to_all(
        jnp.broadcast_to(squares[None], (32, 8, 128)), ("x", "y", "c"), split_axis=0, concat_axis=0, tiled=True
    )
    return make_clipped(zh.reshape(1), squares, by_value, by_out)


def solution(mesh):
    fine = Mesh(mesh.devices.reshape(SHAPE), AXES)
    rows, member = AXES, AXES[1:]
    return jax.shard_map(
        per_device,
        mesh=fine,
        in_specs=(
            P(rows, None, None),
            P(rows, None, None),
            P(rows, None),
            P(rows),
            P(rows, None),
            P(rows),
            P(rows),
            P(),
            P(member, None),
            P(member, None),
            P(member, None),
            P(member, None),
            P(),
            P(),
        ),
        out_specs=(P(member, None), P(member, None)),
        check_vma=False,
    )
```

```python
import jax
import jax.numpy as jnp
from jax import lax
from jax.experimental import pallas as pl
from jax.experimental.pallas import tpu as pltpu
from jax.sharding import Mesh
from jax.sharding import PartitionSpec as P

AXES = ("g", "x", "zh", "y", "c")
SHAPE = (8, 4, 2, 4, 2)
SWAP = [(0, 1), (1, 0)]

HEADS = 4
HEAD_DIM = 128
ACTIONS = 18
STEPS = 24
BLOCKS = 8
BLOCK = 96
PAD = 24
TILES = 13

trace_lambda = 0.95
discount = 0.997
clip_norm = 1024.0

F32 = jnp.float32
BF16 = jnp.bfloat16
HIGHEST = lax.Precision.HIGHEST
VMEM = pl.BlockSpec(memory_space=pltpu.VMEM)
HBM = pl.BlockSpec(memory_space=pltpu.HBM)
SMEM = pl.BlockSpec(memory_space=pltpu.SMEM)


def call(kernel, out_shape, in_specs, scratch=(), flops=0, moved=0, limit=10):
    return pl.pallas_call(
        kernel,
        out_shape=out_shape,
        in_specs=in_specs,
        out_specs=jax.tree.map(lambda s: VMEM, out_shape),
        scratch_shapes=list(scratch),
        compiler_params=pltpu.CompilerParams(vmem_limit_bytes=limit * 1024 * 1024),
        cost_estimate=pl.CostEstimate(flops=flops, bytes_accessed=moved, transcendentals=0),
    )


def shape(dims, dtype=F32):
    return jax.ShapeDtypeStruct(dims, dtype)


def iota(dims, axis):
    return lax.broadcasted_iota(jnp.int32, dims, axis)


def dot_nt(a, b):
    return lax.dot_general(a, b, (((1,), (1,)), ((), ())), preferred_element_type=F32)


def split(values):
    high = values.astype(BF16).astype(F32)
    return high, values - high


def step_of(lanes):
    out = lanes
    for edge in (24, 48, 72, 96, 120):
        out = out - jnp.where(lanes >= edge, 24, 0)
    return out


def stacked_heads(q_turned, policy_turned, rows):
    gap = jnp.zeros((PAD - ACTIONS, 1024), F32)
    parts = [q_turned[...].astype(F32), gap, policy_turned[...].astype(F32), gap]
    if rows > 2 * PAD:
        parts.append(jnp.zeros((rows - 2 * PAD, 1024), F32))
    return jnp.concatenate(parts, axis=0).astype(BF16)


def payload_kernel(
    zh_ref, w_query_at, w_key_at, w_value_at, w_out_at, q_at, policy_at, owner_at, slot_at, weight_at,
    own, copies, keep,
    w_query, w_key, w_value, w_out, q_turned, policy_turned, owner, slot, weight, sems,
):
    pairs = (
        (w_query_at, w_query), (w_key_at, w_key), (w_value_at, w_value),
        (w_out_at, w_out), (q_at, q_turned), (policy_at, policy_turned),
        (owner_at, owner), (slot_at, slot), (weight_at, weight),
    )
    moves = [pltpu.make_async_copy(a, b, sems.at[k]) for k, (a, b) in enumerate(pairs)]
    for move in moves:
        move.start()
    for move in moves:
        move.wait()
    heads = stacked_heads(q_turned, policy_turned, 128)
    high, low = split(dot_nt(w_out[...], heads))
    both = high + pltpu.roll(low, 48, 1)
    last = jnp.concatenate([both, jnp.zeros((8, 128), F32)], axis=0).astype(BF16)
    tiles = [
        ref[:, tile * 128 : (tile + 1) * 128] for ref in (w_query, w_key, w_value) for tile in range(4)
    ] + [last]
    for k, tile in enumerate(tiles):
        own[k] = tile
        for d in range(16):
            copies[d, k] = tile

    member = owner[...]
    code = ((member >> 4) * 8 + (member & 7)) * 32 + slot[...]
    stays = ((member >> 3) & 1) == zh_ref[0]
    diagonal = iota((32, 32), 0) == iota((32, 32), 1)

    def column(lanes):
        return jnp.sum(jnp.where(diagonal, lanes, 0.0), axis=1, keepdims=True)

    at = column(code.astype(F32)).astype(jnp.int32)
    by_row = jnp.where(at >> 7 == iota((32, 8), 1), 1.0, 0.0)
    place = (at & 127) == iota((32, 128), 1)

    def table(weights):
        return lax.dot_general(
            by_row,
            jnp.where(place, column(weights), 0.0),
            (((0,), (0,)), ((), ())),
            preferred_element_type=F32,
            precision=HIGHEST,
        )

    keep[...] = table(jnp.where(stays, weight[...], 0.0))
    high, low = split(table(jnp.where(stays, 0.0, weight[...])))
    own[TILES] = jnp.concatenate([high, low], axis=0).astype(BF16)


def norm_kernel(
    embeds, gain, q_turned, policy_turned, steps, actions, lengths, normed, base, q_rows, aux
):
    both = stacked_heads(q_turned, policy_turned, 48)
    q_rows[...] = jnp.concatenate(
        [jnp.zeros((96, 1024), F32), both[:PAD].astype(F32), jnp.zeros((8, 1024), F32)], axis=0
    )
    base[...] = jnp.zeros_like(base)
    for b in range(BLOCKS):
        rows = embeds[b * BLOCK : (b + 1) * BLOCK, :]
        values = rows.astype(F32)
        meansq = jnp.mean(values * values, axis=-1, keepdims=True)
        normed[b * BLOCK : (b + 1) * BLOCK, :] = (
            values * lax.rsqrt(meansq + 1e-06) * gain[...]
        ).astype(BF16)
        base[b, :, :BLOCK] = dot_nt(both, rows)

    place = iota((STEPS, 128), 1)
    by_step = jnp.where(step_of(place) == iota((STEPS, 128), 0), 1.0, 0.0).astype(BF16)
    seq, lane = iota((32, 128), 0), iota((32, 128), 1)
    real = (seq & 3) * STEPS == lane - step_of(lane)
    block, member = iota((BLOCKS, 32), 0), iota((BLOCKS, 32), 1)
    by_block = jnp.where(member >> 2 == block, 1.0, 0.0)

    def lanes(array):
        wide = lax.dot_general(
            array.astype(BF16), by_step, (((0,), (0,)), ((), ())), preferred_element_type=F32
        )
        return fold(jnp.where(real, wide, 0.0))

    def fold(wide):
        return jnp.dot(by_block.astype(BF16), wide.astype(BF16), preferred_element_type=F32)

    aux[0] = lanes(steps[0])
    aux[1] = jnp.where(iota((BLOCKS, 128), 1) >= BLOCK, 1.0, lanes(steps[1]))
    aux[2] = lanes(actions[...].astype(F32))
    shares = by_block * lengths[...].astype(F32)
    aux[3] = jnp.dot(
        shares.astype(BF16), jnp.where(real, 1.0, 0.0).astype(BF16), preferred_element_type=F32
    )


def pack_kernel(other, keep_at, out, keep, sem):
    move = pltpu.make_async_copy(keep_at, keep, sem)
    move.start()
    for d in range(16):
        for k in range(12):
            out[d, k] = other[k]
    move.wait()
    table = other[TILES].astype(F32)
    high, low = split(keep[...] + table[:8] + table[8:])
    zeros = jnp.zeros((8, 128), F32)
    last = other[12].astype(F32)
    for d in range(16):
        rows = jnp.concatenate(
            [high[d >> 1 : (d >> 1) + 1], low[d >> 1 : (d >> 1) + 1], zeros[:6]], axis=0
        )
        if d & 1:
            rows = pltpu.roll(rows, 64, 1)
        out[d, 12] = (last + jnp.concatenate([zeros, rows], axis=0)).astype(BF16)


def main_kernel(
    place, normed, base, mine_first, theirs_first, mine_last, theirs_last, aux, out, value_rows,
    wall, wo, qkv, probs, mixed, logits, dq, grad_n, grad_g,
):
    zh, c = place[0], place[1]
    sources = (
        (mine_first, zh, c), (theirs_first, zh, 1 - c), (mine_last, 1 - zh, c), (theirs_last, 1 - zh, 1 - c)
    )

    def unpack(s, total):
        x, y = s >> 2, s & 3
        for k, (source, half, core) in enumerate(sources):
            m = ((x * 2 + half) * 4 + y) * 2 + core
            rows = pl.ds(pl.multiple_of(m * 16, 16), 16)
            for tile in range(12):
                wall[rows, tile * 128 : (tile + 1) * 128] = source[s, tile]
            last = source[s, 12].astype(F32)
            wo[pl.ds(pl.multiple_of(m * 8, 8), 8), :] = last[:8]
            if k >= 2:
                total = total + last
        return total

    total = lax.fori_loop(0, 16, unpack, jnp.zeros((16, 128), F32), unroll=2)
    weights = total[8:9] + total[9:10]
    weights = jnp.where(c == 0, weights, pltpu.roll(weights, 96, 1))

    turned = wo[...].T
    both = turned[:96].astype(BF16)
    own_value = turned[:PAD] + turned[48 : 48 + PAD]
    head_of = iota((PAD, 512), 1) >> 7
    for h in range(HEADS):
        value_rows[h * PAD : (h + 1) * PAD, :] = jnp.where(head_of == h, own_value, 0.0)
    value_rows[HEADS * PAD :, :] = jnp.zeros((128 - HEADS * PAD, 512), F32)

    def project(n, carry):
        cols = pl.ds(pl.multiple_of(n * 256, 256), 256)
        qkv[:, cols] = jnp.dot(
            normed[...], wall[:, cols], preferred_element_type=F32
        ).astype(BF16)
        return carry

    lax.fori_loop(0, 6, project, 0, unroll=2)

    row, col = iota((BLOCK, BLOCK), 0), iota((BLOCK, BLOCK), 1)
    row_step, col_step = step_of(row), step_of(col)
    causal = (row - row_step == col - col_step) & (row_step <= col_step)
    logits[...] = base[...]

    def attend(b, carry):
        rows = pl.ds(pl.multiple_of(b * BLOCK, 32), BLOCK)
        lengths = aux[3, pl.ds(b, 1), :][:, :BLOCK].astype(jnp.int32)
        allowed = (causal & (row_step < lengths))[None]
        scores = jnp.stack([
            dot_nt(qkv[rows, 512 + h * 128 : 640 + h * 128], qkv[rows, h * 128 : h * 128 + 128])
            for h in range(HEADS)
        ])
        scores = jnp.where(allowed, scores * HEAD_DIM ** (-0.5), -1e30)
        peak = jnp.max(scores, axis=1, keepdims=True)
        grown = jnp.where(allowed, jnp.exp(scores - peak), 0.0)
        weighed = (grown * (1.0 / jnp.sum(grown, axis=1, keepdims=True))).astype(BF16)
        for h in range(HEADS):
            part = weighed[h].T
            probs[b * HEADS + h] = part
            mixed[rows, h * 128 : h * 128 + 128] = jnp.dot(
                part, qkv[rows, 1024 + h * 128 : 1152 + h * 128], preferred_element_type=F32
            ).astype(BF16)
        lifted = dot_nt(both, mixed[rows, :])
        logits[b, :, :BLOCK] = logits[b, :, :BLOCK] + lifted[:48] + lifted[48:]
        return carry

    lax.fori_loop(0, BLOCKS, attend, 0, unroll=4)

    action_row = iota((BLOCKS, PAD, 128), 1)
    real = action_row < ACTIONS
    qvals = logits[:, :PAD, :]
    raised = jnp.where(real, logits[:, PAD:, :], -1e30)
    raised = jnp.where(real, jnp.exp(raised - jnp.max(raised, axis=1, keepdims=True)), 0.0)
    policy = raised / jnp.sum(raised, axis=1, keepdims=True)
    picked = action_row == aux[2].astype(jnp.int32)[:, None, :]
    values = jnp.sum(policy * qvals, axis=1)
    taken = jnp.sum(jnp.where(picked, qvals, 0.0), axis=1)
    chosen = jnp.sum(jnp.where(picked, policy, 0.0), axis=1)
    behaviour = aux[1]
    traces = trace_lambda * jnp.where(chosen >= behaviour, 1.0, chosen / behaviour)
    lengths = aux[3].astype(jnp.int32)
    lane, block = iota((BLOCKS, 128), 1), iota((BLOCKS, 128), 0)
    step = step_of(lane)
    onward = step + 1 < lengths

    def later(array, count):
        return pltpu.roll(array, 128 - count, 1)

    next_traces = later(traces, 1)
    targets = aux[0] + jnp.where(
        onward, discount * (later(values, 1) - next_traces * later(taken, 1)), 0.0
    )
    factor = jnp.where(onward, discount * next_traces, 0.0)
    for count in (1, 2, 4, 8, 16):
        targets = targets + factor * later(targets, count)
        factor = factor * later(factor, count)

    by_block = jnp.where(lane >> 2 == block, weights, 0.0)
    slot, place = iota((128, 128), 0), iota((128, 128), 1)
    spread = jnp.where((slot & 3) * STEPS == place - step_of(place), 1.0, 0.0)
    row_weight = jnp.dot(by_block, spread, preferred_element_type=F32, precision=HIGHEST)
    live = (step < lengths) & (row_weight != 0.0)
    errors = jnp.where(live, row_weight * (taken - targets), 0.0)
    high, low = split(errors)
    dq[:, :PAD, :] = jnp.where(picked, high[:, None, :], 0.0).astype(BF16)
    dq[:, PAD:, :] = jnp.where(picked, low[:, None, :], 0.0).astype(BF16)

    grad_n[...] = jnp.zeros_like(grad_n)
    grad_g[...] = jnp.zeros_like(grad_g)

    def backward(b, carry):
        rows = pl.ds(pl.multiple_of(b * BLOCK, 32), BLOCK)
        given = dq[b][:, :BLOCK]
        parts = []
        for h in range(HEADS):
            both_parts = jnp.dot(given, probs[b * HEADS + h], preferred_element_type=F32)
            parts.append(both_parts[:PAD] + both_parts[PAD:])
        high, low = split(jnp.concatenate(parts, axis=0))
        stacked = jnp.concatenate([high, low], axis=0).astype(BF16)
        update = jnp.dot(stacked, normed[rows, :], preferred_element_type=F32)
        grad_n[:96, :] += update[:96] + update[96:]
        update = jnp.dot(given, mixed[rows, :], preferred_element_type=F32)
        grad_g[96 : 96 + PAD, :] += update[:PAD] + update[PAD:]
        return carry

    lax.fori_loop(0, BLOCKS, backward, 0, unroll=2)

    by_row, by_feature = grad_n[...].T, grad_g[...].T
    for p in range(32):
        x, y, core = p >> 3, (p >> 1) & 3, p & 1
        m0 = (x * 8 + y) * 2 + core
        m1 = m0 + 8
        upper = by_row[m0 * 16 : m0 * 16 + 16] + jnp.concatenate(
            [by_feature[m0 * 8 : m0 * 8 + 8], by_feature[m1 * 8 : m1 * 8 + 8]], axis=0
        )
        out[p] = jnp.concatenate([upper, by_row[m1 * 16 : m1 * 16 + 16]], axis=0).astype(out.dtype)


def grads_kernel(parts, value_rows, q_rows, grad_value, grad_out, squares):
    total = parts[0].astype(F32)
    for z in range(1, 16):
        total = total + parts[z].astype(F32)
    by_value = jnp.dot(total, value_rows[...], preferred_element_type=F32, precision=HIGHEST)
    by_out = jnp.dot(total[:16], q_rows[...], preferred_element_type=F32, precision=HIGHEST)
    grad_value[...] = by_value
    grad_out[...] = by_out
    sums = jnp.zeros((8, 128), F32)
    for array in (by_value * by_value, by_out * by_out):
        for r in range(0, array.shape[0], 8):
            for k in range(0, array.shape[1], 128):
                sums = sums + array[r : r + 8, k : k + 128]
    squares[...] = sums


def clip_kernel(zh_ref, squares, by_value, by_out, grad_value, grad_out):
    zh = zh_ref[0]
    total = jnp.sum(jnp.sum(squares[...], axis=0), keepdims=True)
    scale = jnp.minimum(1.0, clip_norm / jnp.sqrt(total))
    grad_value[...] = by_value[pl.ds(pl.multiple_of(zh * 16, 16), 16), :] * scale
    grad_out[...] = by_out[pl.ds(pl.multiple_of(zh * 8, 8), 8), :] * scale


def make_payload(zh, w_query, w_key, w_value, w_out, q_turned, policy_turned, owner, slot, weight):
    return call(
        payload_kernel,
        (shape((TILES + 1, 16, 128), BF16), shape((16, TILES, 16, 128), BF16), shape((8, 128))),
        [SMEM] + [HBM] * 9,
        [pltpu.VMEM((16, 512), BF16)] * 3
        + [pltpu.VMEM((8, 1024), BF16)]
        + [pltpu.VMEM((ACTIONS, 1024), BF16)] * 2
        + [pltpu.VMEM((1, 32), jnp.int32)] * 2
        + [pltpu.VMEM((1, 32), F32)]
        + [pltpu.SemaphoreType.DMA((9,))],
        flops=2 * 10**6,
        moved=10**6,
        limit=60,
    )(zh, w_query, w_key, w_value, w_out, q_turned, policy_turned, owner, slot, weight)


def make_normed(embeds, gain, q_turned, policy_turned, steps, actions, lengths):
    return call(
        norm_kernel,
        (
            shape((768, 1024), BF16),
            shape((BLOCKS, 48, 128)),
            shape((128, 1024)),
            shape((4, BLOCKS, 128)),
        ),
        [VMEM] * 7,
        flops=10**8,
        moved=4 * 10**6,
    )(embeds, gain, q_turned, policy_turned, steps, actions, lengths)


def make_message(other, keep):
    return call(
        pack_kernel,
        shape((16, TILES, 16, 128), BF16),
        [VMEM, HBM],
        [pltpu.VMEM((8, 128), F32), pltpu.SemaphoreType.DMA],
        moved=10**6,
    )(other, keep)


def make_sums(place, normed, base, blocks, aux, dtype):
    return call(
        main_kernel,
        (shape((32, 32, 128), dtype), shape((128, 512))),
        [SMEM] + [VMEM] * 7,
        [
            pltpu.VMEM((1024, 1536), BF16),
            pltpu.VMEM((512, 128), F32),
            pltpu.VMEM((768, 1536), BF16),
            pltpu.VMEM((BLOCKS * HEADS, BLOCK, BLOCK), BF16),
            pltpu.VMEM((768, 512), BF16),
            pltpu.VMEM((BLOCKS, 48, 128), F32),
            pltpu.VMEM((BLOCKS, 48, 128), BF16),
            pltpu.VMEM((128, 1024), F32),
            pltpu.VMEM((128, 512), F32),
        ],
        flops=4 * 10**9,
        moved=10**7,
        limit=22,
    )(place, normed, base, *blocks, aux)


def make_grads(parts, value_rows, q_rows):
    return call(
        grads_kernel,
        (shape((32, 512)), shape((16, 1024)), shape((8, 128))),
        [VMEM] * 3,
        flops=10**7,
        moved=10**6,
    )(parts, value_rows, q_rows)


def make_clipped(zh, squares, by_value, by_out):
    return call(
        clip_kernel, (shape((16, 512)), shape((8, 1024))), [SMEM] + [VMEM] * 3, moved=2 * 10**5
    )(zh, squares, by_value, by_out)


def per_device(
    replay_embed,
    replay_steps,
    replay_actions,
    replay_lengths,
    sample_owner,
    sample_slot,
    sample_weight,
    norm_gain,
    w_query,
    w_key,
    w_value,
    w_out,
    q_head,
    policy_head,
):
    zh = lax.axis_index("zh").astype(jnp.int32)
    core = lax.axis_index("c").astype(jnp.int32)
    place = jnp.stack([zh, core])
    q_turned, policy_turned = q_head.T, policy_head.T
    own, copies, keep = make_payload(
        zh.reshape(1),
        w_query,
        w_key,
        w_value,
        w_out,
        q_turned,
        policy_turned,
        sample_owner.reshape(1, 32),
        sample_slot.reshape(1, 32),
        sample_weight.reshape(1, 32),
    )
    other = lax.ppermute(own, "zh", SWAP)
    mine_first = lax.all_to_all(copies, ("x", "y"), split_axis=0, concat_axis=0, tiled=True)
    normed, base, q_rows, aux = make_normed(
        replay_embed.reshape(768, 1024),
        norm_gain.reshape(1, 1024),
        q_turned,
        policy_turned,
        replay_steps.transpose(1, 2, 0),
        replay_actions.T,
        replay_lengths.reshape(1, 32),
    )
    message = make_message(other, keep)
    mine_last = lax.all_to_all(message, ("x", "y"), split_axis=0, concat_axis=0, tiled=True)
    theirs_first = lax.ppermute(mine_first, "c", SWAP)
    theirs_last = lax.ppermute(mine_last, "c", SWAP)
    blocks = (mine_first, theirs_first, mine_last, theirs_last)
    sums, value_rows = make_sums(place, normed, base, blocks, aux, BF16)
    parts = lax.all_to_all(sums, ("x", "y", "c"), split_axis=0, concat_axis=0, tiled=True)
    plane = jnp.sum(parts.astype(F32), axis=0).astype(BF16)
    copies = jnp.broadcast_to(plane[None], (16, 32, 128))
    planes = lax.all_to_all(copies, ("zh", "g"), split_axis=0, concat_axis=0, tiled=True)
    by_value, by_out, squares = make_grads(planes, value_rows, q_rows)
    squares = lax.all_to_all(
        jnp.broadcast_to(squares[None], (32, 8, 128)), ("x", "y", "c"), split_axis=0, concat_axis=0, tiled=True
    )
    return make_clipped(zh.reshape(1), squares, by_value, by_out)


def solution(mesh):
    fine = Mesh(mesh.devices.reshape(SHAPE), AXES)
    rows, member = AXES, AXES[1:]
    return jax.shard_map(
        per_device,
        mesh=fine,
        in_specs=(
            P(rows, None, None),
            P(rows, None, None),
            P(rows, None),
            P(rows),
            P(rows, None),
            P(rows),
            P(rows),
            P(),
            P(member, None),
            P(member, None),
            P(member, None),
            P(member, None),
            P(),
            P(),
        ),
        out_specs=(P(member, None), P(member, None)),
        check_vma=False,
    )
```

```python
import jax
import jax.numpy as jnp
from jax import lax
from jax.experimental import pallas as pl
from jax.experimental.pallas import tpu as pltpu
from jax.sharding import Mesh
from jax.sharding import PartitionSpec as P

AXES = ("g", "x", "zh", "y", "c")
SHAPE = (8, 4, 2, 4, 2)
SWAP = [(0, 1), (1, 0)]

HEADS = 4
HEAD_DIM = 128
ACTIONS = 18
STEPS = 24
BLOCKS = 8
BLOCK = 96
PAD = 24
TILES = 13

trace_lambda = 0.95
discount = 0.997
clip_norm = 1024.0

F32 = jnp.float32
BF16 = jnp.bfloat16
HIGHEST = lax.Precision.HIGHEST
VMEM = pl.BlockSpec(memory_space=pltpu.VMEM)
HBM = pl.BlockSpec(memory_space=pltpu.HBM)
SMEM = pl.BlockSpec(memory_space=pltpu.SMEM)


def call(kernel, out_shape, in_specs, scratch=(), flops=0, moved=0, limit=10):
    return pl.pallas_call(
        kernel,
        out_shape=out_shape,
        in_specs=in_specs,
        out_specs=jax.tree.map(lambda s: VMEM, out_shape),
        scratch_shapes=list(scratch),
        compiler_params=pltpu.CompilerParams(vmem_limit_bytes=limit * 1024 * 1024),
        cost_estimate=pl.CostEstimate(flops=flops, bytes_accessed=moved, transcendentals=0),
    )


def shape(dims, dtype=F32):
    return jax.ShapeDtypeStruct(dims, dtype)


def iota(dims, axis):
    return lax.broadcasted_iota(jnp.int32, dims, axis)


def dot_nt(a, b):
    return lax.dot_general(a, b, (((1,), (1,)), ((), ())), preferred_element_type=F32)


def split(values):
    high = values.astype(BF16).astype(F32)
    return high, values - high


def step_of(lanes):
    out = lanes
    for edge in (24, 48, 72, 96, 120):
        out = out - jnp.where(lanes >= edge, 24, 0)
    return out


def stacked_heads(q_turned, policy_turned, rows):
    gap = jnp.zeros((PAD - ACTIONS, 1024), F32)
    parts = [q_turned[...].astype(F32), gap, policy_turned[...].astype(F32), gap]
    if rows > 2 * PAD:
        parts.append(jnp.zeros((rows - 2 * PAD, 1024), F32))
    return jnp.concatenate(parts, axis=0).astype(BF16)


def payload_kernel(
    zh_ref, w_query_at, w_key_at, w_value_at, w_out_at, q_at, policy_at, owner_at, slot_at, weight_at,
    own, copies, keep,
    w_query, w_key, w_value, w_out, q_turned, policy_turned, owner, slot, weight, sems,
):
    pairs = (
        (w_query_at, w_query), (w_key_at, w_key), (w_value_at, w_value),
        (w_out_at, w_out), (q_at, q_turned), (policy_at, policy_turned),
        (owner_at, owner), (slot_at, slot), (weight_at, weight),
    )
    moves = [pltpu.make_async_copy(a, b, sems.at[k]) for k, (a, b) in enumerate(pairs)]
    for move in moves:
        move.start()
    for move in moves:
        move.wait()
    heads = stacked_heads(q_turned, policy_turned, 128)
    high, low = split(dot_nt(w_out[...], heads))
    both = high + pltpu.roll(low, 48, 1)
    last = jnp.concatenate([both, jnp.zeros((8, 128), F32)], axis=0).astype(BF16)
    tiles = [
        ref[:, tile * 128 : (tile + 1) * 128] for ref in (w_query, w_key, w_value) for tile in range(4)
    ] + [last]
    for k, tile in enumerate(tiles):
        own[k] = tile
        for d in range(16):
            copies[d, k] = tile

    member = owner[...]
    code = ((member >> 4) * 8 + (member & 7)) * 32 + slot[...]
    stays = ((member >> 3) & 1) == zh_ref[0]
    diagonal = iota((32, 32), 0) == iota((32, 32), 1)

    def column(lanes):
        return jnp.sum(jnp.where(diagonal, lanes, 0.0), axis=1, keepdims=True)

    at = column(code.astype(F32)).astype(jnp.int32)
    by_row = jnp.where(at >> 7 == iota((32, 8), 1), 1.0, 0.0)
    place = (at & 127) == iota((32, 128), 1)

    def table(weights):
        return lax.dot_general(
            by_row,
            jnp.where(place, column(weights), 0.0),
            (((0,), (0,)), ((), ())),
            preferred_element_type=F32,
            precision=HIGHEST,
        )

    keep[...] = table(jnp.where(stays, weight[...], 0.0))
    high, low = split(table(jnp.where(stays, 0.0, weight[...])))
    own[TILES] = jnp.concatenate([high, low], axis=0).astype(BF16)


def norm_kernel(
    embeds, gain, q_turned, policy_turned, steps, actions, lengths, normed, base, q_rows, aux
):
    both = stacked_heads(q_turned, policy_turned, 48)
    q_rows[...] = jnp.concatenate(
        [jnp.zeros((96, 1024), F32), both[:PAD].astype(F32), jnp.zeros((8, 1024), F32)], axis=0
    )
    base[...] = jnp.zeros_like(base)
    for b in range(BLOCKS):
        rows = embeds[b * BLOCK : (b + 1) * BLOCK, :]
        values = rows.astype(F32)
        meansq = jnp.mean(values * values, axis=-1, keepdims=True)
        normed[b * BLOCK : (b + 1) * BLOCK, :] = (
            values * lax.rsqrt(meansq + 1e-06) * gain[...]
        ).astype(BF16)
        base[b, :, :BLOCK] = dot_nt(both, rows)

    place = iota((STEPS, 128), 1)
    by_step = jnp.where(step_of(place) == iota((STEPS, 128), 0), 1.0, 0.0).astype(BF16)
    seq, lane = iota((32, 128), 0), iota((32, 128), 1)
    real = (seq & 3) * STEPS == lane - step_of(lane)
    block, member = iota((BLOCKS, 32), 0), iota((BLOCKS, 32), 1)
    by_block = jnp.where(member >> 2 == block, 1.0, 0.0)

    def lanes(array):
        wide = lax.dot_general(
            array.astype(BF16), by_step, (((0,), (0,)), ((), ())), preferred_element_type=F32
        )
        return fold(jnp.where(real, wide, 0.0))

    def fold(wide):
        return jnp.dot(by_block.astype(BF16), wide.astype(BF16), preferred_element_type=F32)

    aux[0] = lanes(steps[0])
    aux[1] = jnp.where(iota((BLOCKS, 128), 1) >= BLOCK, 1.0, lanes(steps[1]))
    aux[2] = lanes(actions[...].astype(F32))
    shares = by_block * lengths[...].astype(F32)
    aux[3] = jnp.dot(
        shares.astype(BF16), jnp.where(real, 1.0, 0.0).astype(BF16), preferred_element_type=F32
    )


def pack_kernel(other, keep_at, out, keep, sem):
    move = pltpu.make_async_copy(keep_at, keep, sem)
    move.start()
    for d in range(16):
        for k in range(12):
            out[d, k] = other[k]
    move.wait()
    table = other[TILES].astype(F32)
    high, low = split(keep[...] + table[:8] + table[8:])
    zeros = jnp.zeros((8, 128), F32)
    last = other[12].astype(F32)
    for d in range(16):
        rows = jnp.concatenate(
            [high[d >> 1 : (d >> 1) + 1], low[d >> 1 : (d >> 1) + 1], zeros[:6]], axis=0
        )
        if d & 1:
            rows = pltpu.roll(rows, 64, 1)
        out[d, 12] = (last + jnp.concatenate([zeros, rows], axis=0)).astype(BF16)


def main_kernel(
    place, normed, base, mine_first, theirs_first, mine_last, theirs_last, aux, out, value_rows,
    wall, wo, qkv, probs, mixed, logits, dq, grad_n, grad_g,
):
    zh, c = place[0], place[1]
    sources = (
        (mine_first, zh, c), (theirs_first, zh, 1 - c), (mine_last, 1 - zh, c), (theirs_last, 1 - zh, 1 - c)
    )

    def unpack(s, total):
        x, y = s >> 2, s & 3
        for k, (source, half, core) in enumerate(sources):
            m = ((x * 2 + half) * 4 + y) * 2 + core
            rows = pl.ds(pl.multiple_of(m * 16, 16), 16)
            for tile in range(12):
                wall[rows, tile * 128 : (tile + 1) * 128] = source[s, tile]
            last = source[s, 12].astype(F32)
            wo[pl.ds(pl.multiple_of(m * 8, 8), 8), :] = last[:8]
            if k >= 2:
                total = total + last
        return total

    total = lax.fori_loop(0, 16, unpack, jnp.zeros((16, 128), F32), unroll=8)
    weights = total[8:9] + total[9:10]
    weights = jnp.where(c == 0, weights, pltpu.roll(weights, 96, 1))

    turned = wo[...].T
    both = turned[:96].astype(BF16)
    own_value = turned[:PAD] + turned[48 : 48 + PAD]
    head_of = iota((PAD, 512), 1) >> 7
    for h in range(HEADS):
        value_rows[h * PAD : (h + 1) * PAD, :] = jnp.where(head_of == h, own_value, 0.0)
    value_rows[HEADS * PAD :, :] = jnp.zeros((128 - HEADS * PAD, 512), F32)

    def project(n, carry):
        cols = pl.ds(pl.multiple_of(n * 256, 256), 256)
        qkv[:, cols] = jnp.dot(
            normed[...], wall[:, cols], preferred_element_type=F32
        ).astype(BF16)
        return carry

    lax.fori_loop(0, 6, project, 0, unroll=6)

    row, col = iota((BLOCK, BLOCK), 0), iota((BLOCK, BLOCK), 1)
    row_step, col_step = step_of(row), step_of(col)
    causal = (row - row_step == col - col_step) & (row_step <= col_step)
    logits[...] = base[...]

    def attend(b, carry):
        rows = pl.ds(pl.multiple_of(b * BLOCK, 32), BLOCK)
        lengths = aux[3, pl.ds(b, 1), :][:, :BLOCK].astype(jnp.int32)
        allowed = (causal & (row_step < lengths))[None]
        scores = jnp.stack([
            dot_nt(qkv[rows, 512 + h * 128 : 640 + h * 128], qkv[rows, h * 128 : h * 128 + 128])
            for h in range(HEADS)
        ])
        scores = jnp.where(allowed, scores * HEAD_DIM ** (-0.5), -1e30)
        peak = jnp.max(scores, axis=1, keepdims=True)
        grown = jnp.where(allowed, jnp.exp(scores - peak), 0.0)
        weighed = (grown * (1.0 / jnp.sum(grown, axis=1, keepdims=True))).astype(BF16)
        for h in range(HEADS):
            part = weighed[h].T
            probs[b * HEADS + h] = part
            mixed[rows, h * 128 : h * 128 + 128] = jnp.dot(
                part, qkv[rows, 1024 + h * 128 : 1152 + h * 128], preferred_element_type=F32
            ).astype(BF16)
        return carry

    lax.fori_loop(0, BLOCKS, attend, 0, unroll=8)

    lifted = dot_nt(both, mixed[...])
    lifted = lifted[:48] + lifted[48:]
    for b in range(BLOCKS):
        logits[b, :, :BLOCK] = logits[b, :, :BLOCK] + lifted[:, b * BLOCK : (b + 1) * BLOCK]

    action_row = iota((BLOCKS, PAD, 128), 1)
    real = action_row < ACTIONS
    qvals = logits[:, :PAD, :]
    raised = jnp.where(real, logits[:, PAD:, :], -1e30)
    raised = jnp.where(real, jnp.exp(raised - jnp.max(raised, axis=1, keepdims=True)), 0.0)
    policy = raised / jnp.sum(raised, axis=1, keepdims=True)
    picked = action_row == aux[2].astype(jnp.int32)[:, None, :]
    values = jnp.sum(policy * qvals, axis=1)
    taken = jnp.sum(jnp.where(picked, qvals, 0.0), axis=1)
    chosen = jnp.sum(jnp.where(picked, policy, 0.0), axis=1)
    behaviour = aux[1]
    traces = trace_lambda * jnp.where(chosen >= behaviour, 1.0, chosen / behaviour)
    lengths = aux[3].astype(jnp.int32)
    lane, block = iota((BLOCKS, 128), 1), iota((BLOCKS, 128), 0)
    step = step_of(lane)
    onward = step + 1 < lengths

    def later(array, count):
        return pltpu.roll(array, 128 - count, 1)

    next_traces = later(traces, 1)
    targets = aux[0] + jnp.where(
        onward, discount * (later(values, 1) - next_traces * later(taken, 1)), 0.0
    )
    factor = jnp.where(onward, discount * next_traces, 0.0)
    for count in (1, 2, 4, 8, 16):
        targets = targets + factor * later(targets, count)
        factor = factor * later(factor, count)

    by_block = jnp.where(lane >> 2 == block, weights, 0.0)
    slot, place = iota((128, 128), 0), iota((128, 128), 1)
    spread = jnp.where((slot & 3) * STEPS == place - step_of(place), 1.0, 0.0)
    row_weight = jnp.dot(by_block, spread, preferred_element_type=F32, precision=HIGHEST)
    live = (step < lengths) & (row_weight != 0.0)
    errors = jnp.where(live, row_weight * (taken - targets), 0.0)
    high, low = split(errors)
    dq[:, :PAD, :] = jnp.where(picked, high[:, None, :], 0.0).astype(BF16)
    dq[:, PAD:, :] = jnp.where(picked, low[:, None, :], 0.0).astype(BF16)

    grad_n[...] = jnp.zeros_like(grad_n)
    grad_g[...] = jnp.zeros_like(grad_g)

    def backward(b, carry):
        rows = pl.ds(b * BLOCK, BLOCK)
        given = dq[b][:, :BLOCK]
        parts = []
        for h in range(HEADS):
            both_parts = jnp.dot(given, probs[b * HEADS + h], preferred_element_type=F32)
            parts.append(both_parts[:PAD] + both_parts[PAD:])
        high, low = split(jnp.concatenate(parts, axis=0))
        stacked = jnp.concatenate([high, low], axis=0).astype(BF16)
        stacks.append(stacked)
        update = jnp.dot(given, mixed[rows, :], preferred_element_type=F32)
        grad_g[96 : 96 + PAD, :] += update[:PAD] + update[PAD:]
        return carry

    stacks = []
    for b in range(BLOCKS):
        backward(b, 0)
    update = jnp.dot(jnp.concatenate(stacks, axis=1), normed[...], preferred_element_type=F32)
    grad_n[:96, :] = update[:96] + update[96:]

    by_row, by_feature = grad_n[...].T, grad_g[...].T
    for p in range(32):
        x, y, core = p >> 3, (p >> 1) & 3, p & 1
        m0 = (x * 8 + y) * 2 + core
        m1 = m0 + 8
        upper = by_row[m0 * 16 : m0 * 16 + 16] + jnp.concatenate(
            [by_feature[m0 * 8 : m0 * 8 + 8], by_feature[m1 * 8 : m1 * 8 + 8]], axis=0
        )
        out[p] = jnp.concatenate([upper, by_row[m1 * 16 : m1 * 16 + 16]], axis=0).astype(out.dtype)


def grads_kernel(parts, value_rows, q_rows, grad_value, grad_out, squares):
    total = parts[0].astype(F32)
    for z in range(1, 16):
        total = total + parts[z].astype(F32)
    by_value = jnp.dot(total, value_rows[...], preferred_element_type=F32, precision=HIGHEST)
    by_out = jnp.dot(total[:16], q_rows[...], preferred_element_type=F32, precision=HIGHEST)
    grad_value[...] = by_value
    grad_out[...] = by_out
    sums = jnp.zeros((8, 128), F32)
    for array in (by_value * by_value, by_out * by_out):
        for r in range(0, array.shape[0], 8):
            for k in range(0, array.shape[1], 128):
                sums = sums + array[r : r + 8, k : k + 128]
    squares[...] = sums


def clip_kernel(zh_ref, squares, by_value, by_out, grad_value, grad_out):
    zh = zh_ref[0]
    total = jnp.sum(jnp.sum(squares[...], axis=0), keepdims=True)
    scale = jnp.minimum(1.0, clip_norm / jnp.sqrt(total))
    grad_value[...] = by_value[pl.ds(pl.multiple_of(zh * 16, 16), 16), :] * scale
    grad_out[...] = by_out[pl.ds(pl.multiple_of(zh * 8, 8), 8), :] * scale


def make_payload(zh, w_query, w_key, w_value, w_out, q_turned, policy_turned, owner, slot, weight):
    return call(
        payload_kernel,
        (shape((TILES + 1, 16, 128), BF16), shape((16, TILES, 16, 128), BF16), shape((8, 128))),
        [SMEM] + [HBM] * 9,
        [pltpu.VMEM((16, 512), BF16)] * 3
        + [pltpu.VMEM((8, 1024), BF16)]
        + [pltpu.VMEM((ACTIONS, 1024), BF16)] * 2
        + [pltpu.VMEM((1, 32), jnp.int32)] * 2
        + [pltpu.VMEM((1, 32), F32)]
        + [pltpu.SemaphoreType.DMA((9,))],
        flops=2 * 10**6,
        moved=10**6,
        limit=60,
    )(zh, w_query, w_key, w_value, w_out, q_turned, policy_turned, owner, slot, weight)


def make_normed(embeds, gain, q_turned, policy_turned, steps, actions, lengths):
    return call(
        norm_kernel,
        (
            shape((768, 1024), BF16),
            shape((BLOCKS, 48, 128)),
            shape((128, 1024)),
            shape((4, BLOCKS, 128)),
        ),
        [VMEM] * 7,
        flops=10**8,
        moved=4 * 10**6,
    )(embeds, gain, q_turned, policy_turned, steps, actions, lengths)


def make_message(other, keep):
    return call(
        pack_kernel,
        shape((16, TILES, 16, 128), BF16),
        [VMEM, HBM],
        [pltpu.VMEM((8, 128), F32), pltpu.SemaphoreType.DMA],
        moved=10**6,
    )(other, keep)


def make_sums(place, normed, base, blocks, aux, dtype):
    return call(
        main_kernel,
        (shape((32, 32, 128), dtype), shape((128, 512))),
        [SMEM] + [VMEM] * 7,
        [
            pltpu.VMEM((1024, 1536), BF16),
            pltpu.VMEM((512, 128), F32),
            pltpu.VMEM((768, 1536), BF16),
            pltpu.VMEM((BLOCKS * HEADS, BLOCK, BLOCK), BF16),
            pltpu.VMEM((768, 512), BF16),
            pltpu.VMEM((BLOCKS, 48, 128), F32),
            pltpu.VMEM((BLOCKS, 48, 128), BF16),
            pltpu.VMEM((128, 1024), F32),
            pltpu.VMEM((128, 512), F32),
        ],
        flops=4 * 10**9,
        moved=10**7,
        limit=22,
    )(place, normed, base, *blocks, aux)


def make_grads(parts, value_rows, q_rows):
    return call(
        grads_kernel,
        (shape((32, 512)), shape((16, 1024)), shape((8, 128))),
        [VMEM] * 3,
        flops=10**7,
        moved=10**6,
    )(parts, value_rows, q_rows)


def make_clipped(zh, squares, by_value, by_out):
    return call(
        clip_kernel, (shape((16, 512)), shape((8, 1024))), [SMEM] + [VMEM] * 3, moved=2 * 10**5
    )(zh, squares, by_value, by_out)


def per_device(
    replay_embed,
    replay_steps,
    replay_actions,
    replay_lengths,
    sample_owner,
    sample_slot,
    sample_weight,
    norm_gain,
    w_query,
    w_key,
    w_value,
    w_out,
    q_head,
    policy_head,
):
    zh = lax.axis_index("zh").astype(jnp.int32)
    core = lax.axis_index("c").astype(jnp.int32)
    place = jnp.stack([zh, core])
    q_turned, policy_turned = q_head.T, policy_head.T
    own, copies, keep = make_payload(
        zh.reshape(1),
        w_query,
        w_key,
        w_value,
        w_out,
        q_turned,
        policy_turned,
        sample_owner.reshape(1, 32),
        sample_slot.reshape(1, 32),
        sample_weight.reshape(1, 32),
    )
    other = lax.ppermute(own, "zh", SWAP)
    mine_first = lax.all_to_all(copies, ("x", "y"), split_axis=0, concat_axis=0, tiled=True)
    normed, base, q_rows, aux = make_normed(
        replay_embed.reshape(768, 1024),
        norm_gain.reshape(1, 1024),
        q_turned,
        policy_turned,
        replay_steps.transpose(1, 2, 0),
        replay_actions.T,
        replay_lengths.reshape(1, 32),
    )
    message = make_message(other, keep)
    mine_last = lax.all_to_all(message, ("x", "y"), split_axis=0, concat_axis=0, tiled=True)
    theirs_first = lax.ppermute(mine_first, "c", SWAP)
    theirs_last = lax.ppermute(mine_last, "c", SWAP)
    blocks = (mine_first, theirs_first, mine_last, theirs_last)
    sums, value_rows = make_sums(place, normed, base, blocks, aux, BF16)
    parts = lax.all_to_all(sums, ("x", "y", "c"), split_axis=0, concat_axis=0, tiled=True)
    plane = jnp.sum(parts.astype(F32), axis=0).astype(BF16)
    copies = jnp.broadcast_to(plane[None], (16, 32, 128))
    planes = lax.all_to_all(copies, ("zh", "g"), split_axis=0, concat_axis=0, tiled=True)
    by_value, by_out, squares = make_grads(planes, value_rows, q_rows)
    squares = lax.all_to_all(
        jnp.broadcast_to(squares[None], (32, 8, 128)), ("x", "y", "c"), split_axis=0, concat_axis=0, tiled=True
    )
    return make_clipped(zh.reshape(1), squares, by_value, by_out)


def solution(mesh):
    fine = Mesh(mesh.devices.reshape(SHAPE), AXES)
    rows, member = AXES, AXES[1:]
    return jax.shard_map(
        per_device,
        mesh=fine,
        in_specs=(
            P(rows, None, None),
            P(rows, None, None),
            P(rows, None),
            P(rows),
            P(rows, None),
            P(rows),
            P(rows),
            P(),
            P(member, None),
            P(member, None),
            P(member, None),
            P(member, None),
            P(),
            P(),
        ),
        out_specs=(P(member, None), P(member, None)),
        check_vma=False,
    )
```

```python
import jax
import jax.numpy as jnp
from jax import lax
from jax.experimental import pallas as pl
from jax.experimental.pallas import tpu as pltpu
from jax.sharding import Mesh
from jax.sharding import PartitionSpec as P

AXES = ("g", "x", "zh", "y", "c")
SHAPE = (8, 4, 2, 4, 2)
SWAP = [(0, 1), (1, 0)]

HEADS = 4
HEAD_DIM = 128
ACTIONS = 18
STEPS = 24
BLOCKS = 8
BLOCK = 96
PAD = 24
TILES = 13

trace_lambda = 0.95
discount = 0.997
clip_norm = 1024.0

F32 = jnp.float32
BF16 = jnp.bfloat16
HIGHEST = lax.Precision.HIGHEST
VMEM = pl.BlockSpec(memory_space=pltpu.VMEM)
HBM = pl.BlockSpec(memory_space=pltpu.HBM)
SMEM = pl.BlockSpec(memory_space=pltpu.SMEM)


def call(kernel, out_shape, in_specs, scratch=(), flops=0, moved=0, limit=10):
    return pl.pallas_call(
        kernel,
        out_shape=out_shape,
        in_specs=in_specs,
        out_specs=jax.tree.map(lambda s: VMEM, out_shape),
        scratch_shapes=list(scratch),
        compiler_params=pltpu.CompilerParams(vmem_limit_bytes=limit * 1024 * 1024),
        cost_estimate=pl.CostEstimate(flops=flops, bytes_accessed=moved, transcendentals=0),
    )


def shape(dims, dtype=F32):
    return jax.ShapeDtypeStruct(dims, dtype)


def iota(dims, axis):
    return lax.broadcasted_iota(jnp.int32, dims, axis)


def dot_nt(a, b):
    return lax.dot_general(a, b, (((1,), (1,)), ((), ())), preferred_element_type=F32)


def split(values):
    high = values.astype(BF16).astype(F32)
    return high, values - high


def step_of(lanes):
    out = lanes
    for edge in (24, 48, 72, 96, 120):
        out = out - jnp.where(lanes >= edge, 24, 0)
    return out


def stacked_heads(q_turned, policy_turned, rows):
    gap = jnp.zeros((PAD - ACTIONS, 1024), F32)
    parts = [q_turned[...].astype(F32), gap, policy_turned[...].astype(F32), gap]
    if rows > 2 * PAD:
        parts.append(jnp.zeros((rows - 2 * PAD, 1024), F32))
    return jnp.concatenate(parts, axis=0).astype(BF16)


def payload_kernel(
    zh_ref, w_query_at, w_key_at, w_value_at, w_out_at, q_at, policy_at, owner_at, slot_at, weight_at,
    own, copies, keep,
    w_query, w_key, w_value, w_out, q_turned, policy_turned, owner, slot, weight, sems,
):
    pairs = (
        (w_query_at, w_query), (w_key_at, w_key), (w_value_at, w_value),
        (w_out_at, w_out), (q_at, q_turned), (policy_at, policy_turned),
        (owner_at, owner), (slot_at, slot), (weight_at, weight),
    )
    moves = [pltpu.make_async_copy(a, b, sems.at[k]) for k, (a, b) in enumerate(pairs)]
    for move in moves:
        move.start()
    for move in moves:
        move.wait()
    heads = stacked_heads(q_turned, policy_turned, 128)
    high, low = split(dot_nt(w_out[...], heads))
    both = high + pltpu.roll(low, 48, 1)
    last = jnp.concatenate([both, jnp.zeros((8, 128), F32)], axis=0).astype(BF16)
    tiles = [
        ref[:, tile * 128 : (tile + 1) * 128] for ref in (w_query, w_key, w_value) for tile in range(4)
    ] + [last]
    for k, tile in enumerate(tiles):
        own[k] = tile
        for d in range(16):
            copies[d, k] = tile

    member = owner[...]
    code = ((member >> 4) * 8 + (member & 7)) * 32 + slot[...]
    stays = ((member >> 3) & 1) == zh_ref[0]
    diagonal = iota((32, 32), 0) == iota((32, 32), 1)

    def column(lanes):
        return jnp.sum(jnp.where(diagonal, lanes, 0.0), axis=1, keepdims=True)

    at = column(code.astype(F32)).astype(jnp.int32)
    by_row = jnp.where(at >> 7 == iota((32, 8), 1), 1.0, 0.0)
    place = (at & 127) == iota((32, 128), 1)

    def table(weights):
        return lax.dot_general(
            by_row,
            jnp.where(place, column(weights), 0.0),
            (((0,), (0,)), ((), ())),
            preferred_element_type=F32,
            precision=HIGHEST,
        )

    keep[...] = table(jnp.where(stays, weight[...], 0.0))
    high, low = split(table(jnp.where(stays, 0.0, weight[...])))
    own[TILES] = jnp.concatenate([high, low], axis=0).astype(BF16)


def norm_kernel(
    embeds, gain, q_turned, policy_turned, steps, actions, lengths, normed, base, q_rows, aux
):
    both = stacked_heads(q_turned, policy_turned, 48)
    q_rows[...] = jnp.concatenate(
        [jnp.zeros((96, 1024), F32), both[:PAD].astype(F32), jnp.zeros((8, 1024), F32)], axis=0
    )
    base[...] = jnp.zeros_like(base)
    for b in range(BLOCKS):
        rows = embeds[b * BLOCK : (b + 1) * BLOCK, :]
        values = rows.astype(F32)
        meansq = jnp.mean(values * values, axis=-1, keepdims=True)
        normed[b * BLOCK : (b + 1) * BLOCK, :] = (
            values * lax.rsqrt(meansq + 1e-06) * gain[...]
        ).astype(BF16)
        base[b, :, :BLOCK] = dot_nt(both, rows)

    place = iota((STEPS, 128), 1)
    by_step = jnp.where(step_of(place) == iota((STEPS, 128), 0), 1.0, 0.0).astype(BF16)
    seq, lane = iota((32, 128), 0), iota((32, 128), 1)
    real = (seq & 3) * STEPS == lane - step_of(lane)
    block, member = iota((BLOCKS, 32), 0), iota((BLOCKS, 32), 1)
    by_block = jnp.where(member >> 2 == block, 1.0, 0.0)

    def lanes(array):
        wide = lax.dot_general(
            array.astype(BF16), by_step, (((0,), (0,)), ((), ())), preferred_element_type=F32
        )
        return fold(jnp.where(real, wide, 0.0))

    def fold(wide):
        return jnp.dot(by_block.astype(BF16), wide.astype(BF16), preferred_element_type=F32)

    aux[0] = lanes(steps[0])
    aux[1] = jnp.where(iota((BLOCKS, 128), 1) >= BLOCK, 1.0, lanes(steps[1]))
    aux[2] = lanes(actions[...].astype(F32))
    shares = by_block * lengths[...].astype(F32)
    aux[3] = jnp.dot(
        shares.astype(BF16), jnp.where(real, 1.0, 0.0).astype(BF16), preferred_element_type=F32
    )


def pack_kernel(other, keep_at, out, keep, sem):
    move = pltpu.make_async_copy(keep_at, keep, sem)
    move.start()
    for d in range(16):
        for k in range(12):
            out[d, k] = other[k]
    move.wait()
    table = other[TILES].astype(F32)
    high, low = split(keep[...] + table[:8] + table[8:])
    zeros = jnp.zeros((8, 128), F32)
    last = other[12].astype(F32)
    for d in range(16):
        rows = jnp.concatenate(
            [high[d >> 1 : (d >> 1) + 1], low[d >> 1 : (d >> 1) + 1], zeros[:6]], axis=0
        )
        if d & 1:
            rows = pltpu.roll(rows, 64, 1)
        out[d, 12] = (last + jnp.concatenate([zeros, rows], axis=0)).astype(BF16)


def main_kernel(
    place, normed, base, mine_first, theirs_first, mine_last, theirs_last, aux, out, value_rows,
    wall, wo, qkv, probs, mixed, logits, dq, grad_n, grad_g,
):
    zh, c = place[0], place[1]
    sources = (
        (mine_first, zh, c), (theirs_first, zh, 1 - c), (mine_last, 1 - zh, c), (theirs_last, 1 - zh, 1 - c)
    )

    def unpack(s, total):
        x, y = s >> 2, s & 3
        for k, (source, half, core) in enumerate(sources):
            m = ((x * 2 + half) * 4 + y) * 2 + core
            rows = pl.ds(pl.multiple_of(m * 16, 16), 16)
            for tile in range(12):
                wall[rows, tile * 128 : (tile + 1) * 128] = source[s, tile]
            last = source[s, 12].astype(F32)
            wo[pl.ds(pl.multiple_of(m * 8, 8), 8), :] = last[:8]
            if k >= 2:
                total = total + last
        return total

    total = lax.fori_loop(0, 16, unpack, jnp.zeros((16, 128), F32), unroll=8)
    weights = total[8:9] + total[9:10]
    weights = jnp.where(c == 0, weights, pltpu.roll(weights, 96, 1))

    turned = wo[...].T
    both = turned[:96].astype(BF16)
    own_value = turned[:PAD] + turned[48 : 48 + PAD]
    head_of = iota((PAD, 512), 1) >> 7
    for h in range(HEADS):
        value_rows[h * PAD : (h + 1) * PAD, :] = jnp.where(head_of == h, own_value, 0.0)
    value_rows[HEADS * PAD :, :] = jnp.zeros((128 - HEADS * PAD, 512), F32)

    def project(n, carry):
        cols = pl.ds(pl.multiple_of(n * 256, 256), 256)
        qkv[:, cols] = jnp.dot(
            normed[...], wall[:, cols], preferred_element_type=F32
        ).astype(BF16)
        return carry

    lax.fori_loop(0, 6, project, 0, unroll=6)

    row, col = iota((BLOCK, BLOCK), 0), iota((BLOCK, BLOCK), 1)
    row_step, col_step = step_of(row), step_of(col)
    causal = (row - row_step == col - col_step) & (row_step <= col_step)
    logits[...] = base[...]

    def attend(b, carry):
        rows = pl.ds(pl.multiple_of(b * BLOCK, 32), BLOCK)
        lengths = aux[3, pl.ds(b, 1), :][:, :BLOCK].astype(jnp.int32)
        allowed = (causal & (row_step < lengths))[None]
        scores = jnp.stack([
            dot_nt(qkv[rows, 512 + h * 128 : 640 + h * 128], qkv[rows, h * 128 : h * 128 + 128])
            for h in range(HEADS)
        ])
        scores = jnp.where(allowed, scores * HEAD_DIM ** (-0.5), -1e30)
        peak = jnp.max(scores, axis=1, keepdims=True)
        grown = jnp.where(allowed, jnp.exp(scores - peak), 0.0)
        weighed = (grown * (1.0 / jnp.sum(grown, axis=1, keepdims=True))).astype(BF16)
        for h in range(HEADS):
            part = weighed[h].T
            probs[b * HEADS + h] = part
            mixed[rows, h * 128 : h * 128 + 128] = jnp.dot(
                part, qkv[rows, 1024 + h * 128 : 1152 + h * 128], preferred_element_type=F32
            ).astype(BF16)
        return carry

    lax.fori_loop(0, BLOCKS, attend, 0, unroll=8)

    lifted = dot_nt(both, mixed[...])
    lifted = lifted[:48] + lifted[48:]
    for b in range(BLOCKS):
        logits[b, :, :BLOCK] = logits[b, :, :BLOCK] + lifted[:, b * BLOCK : (b + 1) * BLOCK]

    action_row = iota((BLOCKS, PAD, 128), 1)
    real = action_row < ACTIONS
    qvals = logits[:, :PAD, :]
    raised = jnp.where(real, logits[:, PAD:, :], -1e30)
    raised = jnp.where(real, jnp.exp(raised - jnp.max(raised, axis=1, keepdims=True)), 0.0)
    policy = raised / jnp.sum(raised, axis=1, keepdims=True)
    picked = action_row == aux[2].astype(jnp.int32)[:, None, :]
    values = jnp.sum(policy * qvals, axis=1)
    taken = jnp.sum(jnp.where(picked, qvals, 0.0), axis=1)
    chosen = jnp.sum(jnp.where(picked, policy, 0.0), axis=1)
    behaviour = aux[1]
    traces = trace_lambda * jnp.where(chosen >= behaviour, 1.0, chosen / behaviour)
    lengths = aux[3].astype(jnp.int32)
    lane, block = iota((BLOCKS, 128), 1), iota((BLOCKS, 128), 0)
    step = step_of(lane)
    onward = step + 1 < lengths

    def later(array, count):
        return pltpu.roll(array, 128 - count, 1)

    next_traces = later(traces, 1)
    targets = aux[0] + jnp.where(
        onward, discount * (later(values, 1) - next_traces * later(taken, 1)), 0.0
    )
    factor = jnp.where(onward, discount * next_traces, 0.0)
    for count in (1, 2, 4, 8, 16):
        targets = targets + factor * later(targets, count)
        factor = factor * later(factor, count)

    by_block = jnp.where(lane >> 2 == block, weights, 0.0)
    slot, place = iota((128, 128), 0), iota((128, 128), 1)
    spread = jnp.where((slot & 3) * STEPS == place - step_of(place), 1.0, 0.0)
    row_weight = jnp.dot(by_block, spread, preferred_element_type=F32, precision=HIGHEST)
    live = (step < lengths) & (row_weight != 0.0)
    errors = jnp.where(live, row_weight * (taken - targets), 0.0)
    high, low = split(errors)
    dq[:, :PAD, :] = jnp.where(picked, high[:, None, :], 0.0).astype(BF16)
    dq[:, PAD:, :] = jnp.where(picked, low[:, None, :], 0.0).astype(BF16)

    grad_n[...] = jnp.zeros_like(grad_n)
    grad_g[...] = jnp.zeros_like(grad_g)

    def backward(b, carry):
        rows = pl.ds(b * BLOCK, BLOCK)
        given = dq[b][:, :BLOCK]
        parts = []
        for h in range(HEADS):
            both_parts = jnp.dot(given, probs[b * HEADS + h], preferred_element_type=F32)
            parts.append(both_parts[:PAD] + both_parts[PAD:])
        high, low = split(jnp.concatenate(parts, axis=0))
        stacked = jnp.concatenate([high, low], axis=0).astype(BF16)
        stacks.append(stacked)
        update = jnp.dot(given, mixed[rows, :], preferred_element_type=F32)
        grad_g[96 : 96 + PAD, :] += update[:PAD] + update[PAD:]
        return carry

    stacks = []
    for b in range(BLOCKS):
        backward(b, 0)
    update = jnp.dot(jnp.concatenate(stacks, axis=1), normed[...], preferred_element_type=F32)
    grad_n[:96, :] = update[:96] + update[96:]

    by_row, by_feature = grad_n[...].T, grad_g[...].T
    for p in range(32):
        x, y, core = p >> 3, (p >> 1) & 3, p & 1
        m0 = (x * 8 + y) * 2 + core
        m1 = m0 + 8
        upper = by_row[m0 * 16 : m0 * 16 + 16] + jnp.concatenate(
            [by_feature[m0 * 8 : m0 * 8 + 8], by_feature[m1 * 8 : m1 * 8 + 8]], axis=0
        )
        out[p] = jnp.concatenate([upper, by_row[m1 * 16 : m1 * 16 + 16]], axis=0).astype(out.dtype)


def grads_kernel(parts, value_rows, q_rows, grad_value, grad_out, squares):
    total = parts[0].astype(F32)
    for z in range(1, 16):
        total = total + parts[z].astype(F32)
    by_value = jnp.dot(total, value_rows[...], preferred_element_type=F32, precision=HIGHEST)
    by_out = jnp.dot(total[:16], q_rows[...], preferred_element_type=F32, precision=HIGHEST)
    grad_value[...] = by_value
    grad_out[...] = by_out
    sums = jnp.zeros((8, 128), F32)
    for array in (by_value * by_value, by_out * by_out):
        for r in range(0, array.shape[0], 8):
            for k in range(0, array.shape[1], 128):
                sums = sums + array[r : r + 8, k : k + 128]
    squares[...] = jnp.sum(sums, axis=0, keepdims=True)


def clip_kernel(zh_ref, squares, by_value, by_out, grad_value, grad_out):
    zh = zh_ref[0]
    total = jnp.sum(jnp.sum(squares[...], axis=0), keepdims=True)
    scale = jnp.minimum(1.0, clip_norm / jnp.sqrt(total))
    grad_value[...] = by_value[pl.ds(pl.multiple_of(zh * 16, 16), 16), :] * scale
    grad_out[...] = by_out[pl.ds(pl.multiple_of(zh * 8, 8), 8), :] * scale


def make_payload(zh, w_query, w_key, w_value, w_out, q_turned, policy_turned, owner, slot, weight):
    return call(
        payload_kernel,
        (shape((TILES + 1, 16, 128), BF16), shape((16, TILES, 16, 128), BF16), shape((8, 128))),
        [SMEM] + [HBM] * 9,
        [pltpu.VMEM((16, 512), BF16)] * 3
        + [pltpu.VMEM((8, 1024), BF16)]
        + [pltpu.VMEM((ACTIONS, 1024), BF16)] * 2
        + [pltpu.VMEM((1, 32), jnp.int32)] * 2
        + [pltpu.VMEM((1, 32), F32)]
        + [pltpu.SemaphoreType.DMA((9,))],
        flops=2 * 10**6,
        moved=10**6,
        limit=60,
    )(zh, w_query, w_key, w_value, w_out, q_turned, policy_turned, owner, slot, weight)


def make_normed(embeds, gain, q_turned, policy_turned, steps, actions, lengths):
    return call(
        norm_kernel,
        (
            shape((768, 1024), BF16),
            shape((BLOCKS, 48, 128)),
            shape((128, 1024)),
            shape((4, BLOCKS, 128)),
        ),
        [VMEM] * 7,
        flops=10**8,
        moved=4 * 10**6,
    )(embeds, gain, q_turned, policy_turned, steps, actions, lengths)


def make_message(other, keep):
    return call(
        pack_kernel,
        shape((16, TILES, 16, 128), BF16),
        [VMEM, HBM],
        [pltpu.VMEM((8, 128), F32), pltpu.SemaphoreType.DMA],
        flops=10**12,
        moved=10**6,
    )(other, keep)


def make_sums(place, normed, base, blocks, aux, dtype):
    return call(
        main_kernel,
        (shape((32, 32, 128), dtype), shape((128, 512))),
        [SMEM] + [VMEM] * 7,
        [
            pltpu.VMEM((1024, 1536), BF16),
            pltpu.VMEM((512, 128), F32),
            pltpu.VMEM((768, 1536), BF16),
            pltpu.VMEM((BLOCKS * HEADS, BLOCK, BLOCK), BF16),
            pltpu.VMEM((768, 512), BF16),
            pltpu.VMEM((BLOCKS, 48, 128), F32),
            pltpu.VMEM((BLOCKS, 48, 128), BF16),
            pltpu.VMEM((128, 1024), F32),
            pltpu.VMEM((128, 512), F32),
        ],
        flops=4 * 10**9,
        moved=10**7,
        limit=22,
    )(place, normed, base, *blocks, aux)


def make_grads(parts, value_rows, q_rows):
    return call(
        grads_kernel,
        (shape((32, 512)), shape((16, 1024)), shape((1, 128))),
        [VMEM] * 3,
        flops=10**7,
        moved=10**6,
    )(parts, value_rows, q_rows)


def make_clipped(zh, squares, by_value, by_out):
    return call(
        clip_kernel, (shape((16, 512)), shape((8, 1024))), [SMEM] + [VMEM] * 3, moved=2 * 10**5
    )(zh, squares, by_value, by_out)


def per_device(
    replay_embed,
    replay_steps,
    replay_actions,
    replay_lengths,
    sample_owner,
    sample_slot,
    sample_weight,
    norm_gain,
    w_query,
    w_key,
    w_value,
    w_out,
    q_head,
    policy_head,
):
    zh = lax.axis_index("zh").astype(jnp.int32)
    core = lax.axis_index("c").astype(jnp.int32)
    place = jnp.stack([zh, core])
    q_turned, policy_turned = q_head.T, policy_head.T
    own, copies, keep = make_payload(
        zh.reshape(1),
        w_query,
        w_key,
        w_value,
        w_out,
        q_turned,
        policy_turned,
        sample_owner.reshape(1, 32),
        sample_slot.reshape(1, 32),
        sample_weight.reshape(1, 32),
    )
    other = lax.ppermute(own, "zh", SWAP)
    mine_first = lax.all_to_all(copies, ("x", "y"), split_axis=0, concat_axis=0, tiled=True)
    normed, base, q_rows, aux = make_normed(
        replay_embed.reshape(768, 1024),
        norm_gain.reshape(1, 1024),
        q_turned,
        policy_turned,
        replay_steps.transpose(1, 2, 0),
        replay_actions.T,
        replay_lengths.reshape(1, 32),
    )
    message = make_message(other, keep)
    mine_last = lax.all_to_all(message, ("x", "y"), split_axis=0, concat_axis=0, tiled=True)
    theirs_first = lax.ppermute(mine_first, "c", SWAP)
    theirs_last = lax.ppermute(mine_last, "c", SWAP)
    blocks = (mine_first, theirs_first, mine_last, theirs_last)
    sums, value_rows = make_sums(place, normed, base, blocks, aux, BF16)
    parts = lax.all_to_all(sums, ("x", "y", "c"), split_axis=0, concat_axis=0, tiled=True)
    plane = jnp.sum(parts.astype(F32), axis=0).astype(BF16)
    copies = jnp.broadcast_to(plane[None], (16, 32, 128))
    planes = lax.all_to_all(copies, ("zh", "g"), split_axis=0, concat_axis=0, tiled=True)
    by_value, by_out, squares = make_grads(planes, value_rows, q_rows)
    squares = lax.all_to_all(
        jnp.broadcast_to(squares[None], (32, 1, 128)), ("x", "y", "c"), split_axis=0, concat_axis=0, tiled=True
    )
    return make_clipped(zh.reshape(1), squares, by_value, by_out)


def solution(mesh):
    fine = Mesh(mesh.devices.reshape(SHAPE), AXES)
    rows, member = AXES, AXES[1:]
    return jax.shard_map(
        per_device,
        mesh=fine,
        in_specs=(
            P(rows, None, None),
            P(rows, None, None),
            P(rows, None),
            P(rows),
            P(rows, None),
            P(rows),
            P(rows),
            P(),
            P(member, None),
            P(member, None),
            P(member, None),
            P(member, None),
            P(),
            P(),
        ),
        out_specs=(P(member, None), P(member, None)),
        check_vma=False,
    )
```

```python
import jax
import jax.numpy as jnp
from jax import lax
from jax.experimental import pallas as pl
from jax.experimental.pallas import tpu as pltpu
from jax.sharding import Mesh
from jax.sharding import PartitionSpec as P

AXES = ("g", "x", "zh", "y", "c")
SHAPE = (8, 4, 2, 4, 2)
SWAP = [(0, 1), (1, 0)]

HEADS = 4
HEAD_DIM = 128
ACTIONS = 18
STEPS = 24
BLOCKS = 8
BLOCK = 96
PAD = 24
TILES = 13

trace_lambda = 0.95
discount = 0.997
clip_norm = 1024.0

F32 = jnp.float32
BF16 = jnp.bfloat16
HIGHEST = lax.Precision.HIGHEST
VMEM = pl.BlockSpec(memory_space=pltpu.VMEM)
HBM = pl.BlockSpec(memory_space=pltpu.HBM)
SMEM = pl.BlockSpec(memory_space=pltpu.SMEM)


def call(kernel, out_shape, in_specs, scratch=(), flops=0, moved=0, limit=10):
    return pl.pallas_call(
        kernel,
        out_shape=out_shape,
        in_specs=in_specs,
        out_specs=jax.tree.map(lambda s: VMEM, out_shape),
        scratch_shapes=list(scratch),
        compiler_params=pltpu.CompilerParams(vmem_limit_bytes=limit * 1024 * 1024),
        cost_estimate=pl.CostEstimate(flops=flops, bytes_accessed=moved, transcendentals=0),
    )


def shape(dims, dtype=F32):
    return jax.ShapeDtypeStruct(dims, dtype)


def iota(dims, axis):
    return lax.broadcasted_iota(jnp.int32, dims, axis)


def dot_nt(a, b):
    return lax.dot_general(a, b, (((1,), (1,)), ((), ())), preferred_element_type=F32)


def split(values):
    high = values.astype(BF16).astype(F32)
    return high, values - high


def step_of(lanes):
    out = lanes
    for edge in (24, 48, 72, 96, 120):
        out = out - jnp.where(lanes >= edge, 24, 0)
    return out


def stacked_heads(q_turned, policy_turned, rows):
    gap = jnp.zeros((PAD - ACTIONS, 1024), F32)
    parts = [q_turned[...].astype(F32), gap, policy_turned[...].astype(F32), gap]
    if rows > 2 * PAD:
        parts.append(jnp.zeros((rows - 2 * PAD, 1024), F32))
    return jnp.concatenate(parts, axis=0).astype(BF16)


def payload_kernel(
    zh_ref, w_query_at, w_key_at, w_value_at, w_out, q_turned, policy_turned, owner_at, slot_at, weight_at,
    own, copies, keep,
    w_query, w_key, w_value, owner, slot, weight, sems,
):
    pairs = (
        (w_query_at, w_query), (w_key_at, w_key), (w_value_at, w_value),
        (owner_at, owner), (slot_at, slot), (weight_at, weight),
    )
    moves = [pltpu.make_async_copy(a, b, sems.at[k]) for k, (a, b) in enumerate(pairs)]
    for move in moves:
        move.start()
    for move in moves:
        move.wait()
    heads = stacked_heads(q_turned, policy_turned, 128)
    high, low = split(dot_nt(w_out[...], heads))
    both = high + pltpu.roll(low, 48, 1)
    last = jnp.concatenate([both, jnp.zeros((8, 128), F32)], axis=0).astype(BF16)
    tiles = [
        ref[:, tile * 128 : (tile + 1) * 128] for ref in (w_query, w_key, w_value) for tile in range(4)
    ] + [last]
    for k, tile in enumerate(tiles):
        own[k] = tile
        for d in range(16):
            copies[d, k] = tile

    member = owner[...]
    code = ((member >> 4) * 8 + (member & 7)) * 32 + slot[...]
    stays = ((member >> 3) & 1) == zh_ref[0]
    diagonal = iota((32, 32), 0) == iota((32, 32), 1)

    def column(lanes):
        return jnp.sum(jnp.where(diagonal, lanes, 0.0), axis=1, keepdims=True)

    at = column(code.astype(F32)).astype(jnp.int32)
    by_row = jnp.where(at >> 7 == iota((32, 8), 1), 1.0, 0.0)
    place = (at & 127) == iota((32, 128), 1)

    def table(weights):
        return lax.dot_general(
            by_row,
            jnp.where(place, column(weights), 0.0),
            (((0,), (0,)), ((), ())),
            preferred_element_type=F32,
            precision=HIGHEST,
        )

    keep[...] = table(jnp.where(stays, weight[...], 0.0))
    high, low = split(table(jnp.where(stays, 0.0, weight[...])))
    own[TILES] = jnp.concatenate([high, low], axis=0).astype(BF16)


def norm_kernel(
    embeds, gain, q_turned, policy_turned, steps, actions, lengths, normed, base, q_rows, aux
):
    both = stacked_heads(q_turned, policy_turned, 48)
    q_rows[...] = jnp.concatenate(
        [jnp.zeros((96, 1024), F32), both[:PAD].astype(F32), jnp.zeros((8, 1024), F32)], axis=0
    )
    base[...] = jnp.zeros_like(base)
    for b in range(BLOCKS):
        rows = embeds[b * BLOCK : (b + 1) * BLOCK, :]
        values = rows.astype(F32)
        meansq = jnp.mean(values * values, axis=-1, keepdims=True)
        normed[b * BLOCK : (b + 1) * BLOCK, :] = (
            values * lax.rsqrt(meansq + 1e-06) * gain[...]
        ).astype(BF16)
        base[b, :, :BLOCK] = dot_nt(both, rows)

    place = iota((STEPS, 128), 1)
    by_step = jnp.where(step_of(place) == iota((STEPS, 128), 0), 1.0, 0.0).astype(BF16)
    seq, lane = iota((32, 128), 0), iota((32, 128), 1)
    real = (seq & 3) * STEPS == lane - step_of(lane)
    block, member = iota((BLOCKS, 32), 0), iota((BLOCKS, 32), 1)
    by_block = jnp.where(member >> 2 == block, 1.0, 0.0)

    def lanes(array):
        wide = lax.dot_general(
            array.astype(BF16), by_step, (((0,), (0,)), ((), ())), preferred_element_type=F32
        )
        return fold(jnp.where(real, wide, 0.0))

    def fold(wide):
        return jnp.dot(by_block.astype(BF16), wide.astype(BF16), preferred_element_type=F32)

    aux[0] = lanes(steps[0])
    aux[1] = jnp.where(iota((BLOCKS, 128), 1) >= BLOCK, 1.0, lanes(steps[1]))
    aux[2] = lanes(actions[...].astype(F32))
    shares = by_block * lengths[...].astype(F32)
    aux[3] = jnp.dot(
        shares.astype(BF16), jnp.where(real, 1.0, 0.0).astype(BF16), preferred_element_type=F32
    )


def pack_kernel(other, keep_at, out, keep, sem):
    move = pltpu.make_async_copy(keep_at, keep, sem)
    move.start()
    for d in range(16):
        for k in range(12):
            out[d, k] = other[k]
    move.wait()
    table = other[TILES].astype(F32)
    high, low = split(keep[...] + table[:8] + table[8:])
    zeros = jnp.zeros((8, 128), F32)
    last = other[12].astype(F32)
    for d in range(16):
        rows = jnp.concatenate(
            [high[d >> 1 : (d >> 1) + 1], low[d >> 1 : (d >> 1) + 1], zeros[:6]], axis=0
        )
        if d & 1:
            rows = pltpu.roll(rows, 64, 1)
        out[d, 12] = (last + jnp.concatenate([zeros, rows], axis=0)).astype(BF16)


def main_kernel(
    place, normed, base, mine_first, theirs_first, mine_last, theirs_last, aux, out, value_rows,
    wall, wo, qkv, probs, mixed, logits, dq, grad_n, grad_g,
):
    zh, c = place[0], place[1]
    sources = (
        (mine_first, zh, c), (theirs_first, zh, 1 - c), (mine_last, 1 - zh, c), (theirs_last, 1 - zh, 1 - c)
    )

    def unpack(s, total):
        x, y = s >> 2, s & 3
        for k, (source, half, core) in enumerate(sources):
            m = ((x * 2 + half) * 4 + y) * 2 + core
            rows = pl.ds(pl.multiple_of(m * 16, 16), 16)
            for tile in range(12):
                wall[rows, tile * 128 : (tile + 1) * 128] = source[s, tile]
            last = source[s, 12].astype(F32)
            wo[pl.ds(pl.multiple_of(m * 8, 8), 8), :] = last[:8]
            if k >= 2:
                total = total + last
        return total

    total = lax.fori_loop(0, 16, unpack, jnp.zeros((16, 128), F32), unroll=8)
    weights = total[8:9] + total[9:10]
    weights = jnp.where(c == 0, weights, pltpu.roll(weights, 96, 1))

    turned = wo[...].T
    both = turned[:96].astype(BF16)
    own_value = turned[:PAD] + turned[48 : 48 + PAD]
    head_of = iota((PAD, 512), 1) >> 7
    for h in range(HEADS):
        value_rows[h * PAD : (h + 1) * PAD, :] = jnp.where(head_of == h, own_value, 0.0)
    value_rows[HEADS * PAD :, :] = jnp.zeros((128 - HEADS * PAD, 512), F32)

    def project(n, carry):
        cols = pl.ds(pl.multiple_of(n * 256, 256), 256)
        qkv[:, cols] = jnp.dot(
            normed[...], wall[:, cols], preferred_element_type=F32
        ).astype(BF16)
        return carry

    lax.fori_loop(0, 6, project, 0, unroll=6)

    row, col = iota((BLOCK, BLOCK), 0), iota((BLOCK, BLOCK), 1)
    row_step, col_step = step_of(row), step_of(col)
    causal = (row - row_step == col - col_step) & (row_step <= col_step)
    logits[...] = base[...]

    def attend(b, carry):
        rows = pl.ds(pl.multiple_of(b * BLOCK, 32), BLOCK)
        lengths = aux[3, pl.ds(b, 1), :][:, :BLOCK].astype(jnp.int32)
        allowed = (causal & (row_step < lengths))[None]
        scores = jnp.stack([
            dot_nt(qkv[rows, 512 + h * 128 : 640 + h * 128], qkv[rows, h * 128 : h * 128 + 128])
            for h in range(HEADS)
        ])
        scores = jnp.where(allowed, scores * HEAD_DIM ** (-0.5), -1e30)
        peak = jnp.max(scores, axis=1, keepdims=True)
        grown = jnp.where(allowed, jnp.exp(scores - peak), 0.0)
        weighed = (grown * (1.0 / jnp.sum(grown, axis=1, keepdims=True))).astype(BF16)
        for h in range(HEADS):
            part = weighed[h].T
            probs[b * HEADS + h] = part
            mixed[rows, h * 128 : h * 128 + 128] = jnp.dot(
                part, qkv[rows, 1024 + h * 128 : 1152 + h * 128], preferred_element_type=F32
            ).astype(BF16)
        return carry

    lax.fori_loop(0, BLOCKS, attend, 0, unroll=8)

    lifted = dot_nt(both, mixed[...])
    lifted = lifted[:48] + lifted[48:]
    for b in range(BLOCKS):
        logits[b, :, :BLOCK] = logits[b, :, :BLOCK] + lifted[:, b * BLOCK : (b + 1) * BLOCK]

    action_row = iota((BLOCKS, PAD, 128), 1)
    real = action_row < ACTIONS
    qvals = logits[:, :PAD, :]
    raised = jnp.where(real, logits[:, PAD:, :], -1e30)
    raised = jnp.where(real, jnp.exp(raised - jnp.max(raised, axis=1, keepdims=True)), 0.0)
    policy = raised / jnp.sum(raised, axis=1, keepdims=True)
    picked = action_row == aux[2].astype(jnp.int32)[:, None, :]
    values = jnp.sum(policy * qvals, axis=1)
    taken = jnp.sum(jnp.where(picked, qvals, 0.0), axis=1)
    chosen = jnp.sum(jnp.where(picked, policy, 0.0), axis=1)
    behaviour = aux[1]
    traces = trace_lambda * jnp.where(chosen >= behaviour, 1.0, chosen / behaviour)
    lengths = aux[3].astype(jnp.int32)
    lane, block = iota((BLOCKS, 128), 1), iota((BLOCKS, 128), 0)
    step = step_of(lane)
    onward = step + 1 < lengths

    def later(array, count):
        return pltpu.roll(array, 128 - count, 1)

    next_traces = later(traces, 1)
    targets = aux[0] + jnp.where(
        onward, discount * (later(values, 1) - next_traces * later(taken, 1)), 0.0
    )
    factor = jnp.where(onward, discount * next_traces, 0.0)
    for count in (1, 2, 4, 8, 16):
        targets = targets + factor * later(targets, count)
        factor = factor * later(factor, count)

    by_block = jnp.where(lane >> 2 == block, weights, 0.0)
    slot, place = iota((128, 128), 0), iota((128, 128), 1)
    spread = jnp.where((slot & 3) * STEPS == place - step_of(place), 1.0, 0.0)
    row_weight = jnp.dot(by_block, spread, preferred_element_type=F32, precision=HIGHEST)
    live = (step < lengths) & (row_weight != 0.0)
    errors = jnp.where(live, row_weight * (taken - targets), 0.0)
    high, low = split(errors)
    dq[...] = jnp.concatenate(
        [jnp.where(picked, high[:, None, :], 0.0), jnp.where(picked, low[:, None, :], 0.0)], axis=1
    ).astype(BF16)

    grad_n[...] = jnp.zeros_like(grad_n)
    grad_g[...] = jnp.zeros_like(grad_g)

    def backward(b, carry):
        rows = pl.ds(b * BLOCK, BLOCK)
        given = dq[b][:, :BLOCK]
        parts = []
        for h in range(HEADS):
            both_parts = jnp.dot(given, probs[b * HEADS + h], preferred_element_type=F32)
            parts.append(both_parts[:PAD] + both_parts[PAD:])
        high, low = split(jnp.concatenate(parts, axis=0))
        stacked = jnp.concatenate([high, low], axis=0).astype(BF16)
        stacks.append(stacked)
        update = jnp.dot(given, mixed[rows, :], preferred_element_type=F32)
        grad_g[96 : 96 + PAD, :] += update[:PAD] + update[PAD:]
        return carry

    stacks = []
    for b in range(BLOCKS):
        backward(b, 0)
    update = jnp.dot(jnp.concatenate(stacks, axis=1), normed[...], preferred_element_type=F32)
    grad_n[:96, :] = update[:96] + update[96:]

    by_row, by_feature = grad_n[...].T, grad_g[...].T
    for p in range(32):
        x, y, core = p >> 3, (p >> 1) & 3, p & 1
        m0 = (x * 8 + y) * 2 + core
        m1 = m0 + 8
        upper = by_row[m0 * 16 : m0 * 16 + 16] + jnp.concatenate(
            [by_feature[m0 * 8 : m0 * 8 + 8], by_feature[m1 * 8 : m1 * 8 + 8]], axis=0
        )
        out[p] = jnp.concatenate([upper, by_row[m1 * 16 : m1 * 16 + 16]], axis=0).astype(out.dtype)


def grads_kernel(parts, value_rows, q_rows, grad_value, grad_out, squares):
    total = parts[0].astype(F32)
    for z in range(1, 16):
        total = total + parts[z].astype(F32)
    by_value = jnp.dot(total, value_rows[...], preferred_element_type=F32, precision=HIGHEST)
    by_out = jnp.dot(total[:16], q_rows[...], preferred_element_type=F32, precision=HIGHEST)
    grad_value[...] = by_value
    grad_out[...] = by_out
    sums = jnp.zeros((8, 128), F32)
    for array in (by_value * by_value, by_out * by_out):
        for r in range(0, array.shape[0], 8):
            for k in range(0, array.shape[1], 128):
                sums = sums + array[r : r + 8, k : k + 128]
    squares[...] = jnp.sum(sums, axis=0, keepdims=True)


def clip_kernel(zh_ref, squares, by_value, by_out, grad_value, grad_out):
    zh = zh_ref[0]
    total = jnp.sum(jnp.sum(squares[...], axis=0), keepdims=True)
    scale = jnp.minimum(1.0, clip_norm / jnp.sqrt(total))
    grad_value[...] = by_value[pl.ds(pl.multiple_of(zh * 16, 16), 16), :] * scale
    grad_out[...] = by_out[pl.ds(pl.multiple_of(zh * 8, 8), 8), :] * scale


def make_payload(zh, w_query, w_key, w_value, w_out, q_turned, policy_turned, owner, slot, weight):
    return call(
        payload_kernel,
        (shape((TILES + 1, 16, 128), BF16), shape((16, TILES, 16, 128), BF16), shape((8, 128))),
        [SMEM] + [HBM] * 3 + [VMEM] * 3 + [HBM] * 3,
        [pltpu.VMEM((16, 512), BF16)] * 3
        + [pltpu.VMEM((1, 32), jnp.int32)] * 2
        + [pltpu.VMEM((1, 32), F32)]
        + [pltpu.SemaphoreType.DMA((6,))],
        flops=2 * 10**6,
        moved=10**6,
        limit=60,
    )(zh, w_query, w_key, w_value, w_out, q_turned, policy_turned, owner, slot, weight)


def make_normed(embeds, gain, q_turned, policy_turned, steps, actions, lengths):
    return call(
        norm_kernel,
        (
            shape((768, 1024), BF16),
            shape((BLOCKS, 48, 128)),
            shape((128, 1024)),
            shape((4, BLOCKS, 128)),
        ),
        [VMEM] * 7,
        flops=10**8,
        moved=4 * 10**6,
    )(embeds, gain, q_turned, policy_turned, steps, actions, lengths)


def make_message(other, keep):
    return call(
        pack_kernel,
        shape((16, TILES, 16, 128), BF16),
        [VMEM, HBM],
        [pltpu.VMEM((8, 128), F32), pltpu.SemaphoreType.DMA],
        flops=10**12,
        moved=10**6,
    )(other, keep)


def make_sums(place, normed, base, blocks, aux, dtype):
    return call(
        main_kernel,
        (shape((32, 32, 128), dtype), shape((128, 512))),
        [SMEM] + [VMEM] * 7,
        [
            pltpu.VMEM((1024, 1536), BF16),
            pltpu.VMEM((512, 128), F32),
            pltpu.VMEM((768, 1536), BF16),
            pltpu.VMEM((BLOCKS * HEADS, BLOCK, BLOCK), BF16),
            pltpu.VMEM((768, 512), BF16),
            pltpu.VMEM((BLOCKS, 48, 128), F32),
            pltpu.VMEM((BLOCKS, 48, 128), BF16),
            pltpu.VMEM((128, 1024), F32),
            pltpu.VMEM((128, 512), F32),
        ],
        flops=4 * 10**9,
        moved=10**7,
        limit=22,
    )(place, normed, base, *blocks, aux)


def make_grads(parts, value_rows, q_rows):
    return call(
        grads_kernel,
        (shape((32, 512)), shape((16, 1024)), shape((1, 128))),
        [VMEM] * 3,
        flops=10**7,
        moved=10**6,
    )(parts, value_rows, q_rows)


def make_clipped(zh, squares, by_value, by_out):
    return call(
        clip_kernel, (shape((16, 512)), shape((8, 1024))), [SMEM] + [VMEM] * 3, moved=2 * 10**5
    )(zh, squares, by_value, by_out)


def per_device(
    replay_embed,
    replay_steps,
    replay_actions,
    replay_lengths,
    sample_owner,
    sample_slot,
    sample_weight,
    norm_gain,
    w_query,
    w_key,
    w_value,
    w_out,
    q_head,
    policy_head,
):
    zh = lax.axis_index("zh").astype(jnp.int32)
    core = lax.axis_index("c").astype(jnp.int32)
    place = jnp.stack([zh, core])
    q_turned, policy_turned = q_head.T, policy_head.T
    own, copies, keep = make_payload(
        zh.reshape(1),
        w_query,
        w_key,
        w_value,
        w_out,
        q_turned,
        policy_turned,
        sample_owner.reshape(1, 32),
        sample_slot.reshape(1, 32),
        sample_weight.reshape(1, 32),
    )
    other = lax.ppermute(own, "zh", SWAP)
    mine_first = lax.all_to_all(copies, ("x", "y"), split_axis=0, concat_axis=0, tiled=True)
    normed, base, q_rows, aux = make_normed(
        replay_embed.reshape(768, 1024),
        norm_gain.reshape(1, 1024),
        q_turned,
        policy_turned,
        replay_steps.transpose(1, 2, 0),
        replay_actions.T,
        replay_lengths.reshape(1, 32),
    )
    message = make_message(other, keep)
    mine_last = lax.all_to_all(message, ("x", "y"), split_axis=0, concat_axis=0, tiled=True)
    theirs_first = lax.ppermute(mine_first, "c", SWAP)
    theirs_last = lax.ppermute(mine_last, "c", SWAP)
    blocks = (mine_first, theirs_first, mine_last, theirs_last)
    sums, value_rows = make_sums(place, normed, base, blocks, aux, BF16)
    parts = lax.all_to_all(sums, ("x", "y", "c"), split_axis=0, concat_axis=0, tiled=True)
    plane = jnp.sum(parts.astype(F32), axis=0).astype(BF16)
    copies = jnp.broadcast_to(plane[None], (16, 32, 128))
    planes = lax.all_to_all(copies, ("zh", "g"), split_axis=0, concat_axis=0, tiled=True)
    by_value, by_out, squares = make_grads(planes, value_rows, q_rows)
    squares = lax.all_to_all(
        jnp.broadcast_to(squares[None], (32, 1, 128)), ("x", "y", "c"), split_axis=0, concat_axis=0, tiled=True
    )
    return make_clipped(zh.reshape(1), squares, by_value, by_out)


def solution(mesh):
    fine = Mesh(mesh.devices.reshape(SHAPE), AXES)
    rows, member = AXES, AXES[1:]
    return jax.shard_map(
        per_device,
        mesh=fine,
        in_specs=(
            P(rows, None, None),
            P(rows, None, None),
            P(rows, None),
            P(rows),
            P(rows, None),
            P(rows),
            P(rows),
            P(),
            P(member, None),
            P(member, None),
            P(member, None),
            P(member, None),
            P(),
            P(),
        ),
        out_specs=(P(member, None), P(member, None)),
        check_vma=False,
    )
```
